32 devices in a mesh: gz: 16 (over z, y, x), gy: 2 (over core).
Axes of the slice: x: 2, y: 2, z: 4, core: 2. Of those that a mesh axis runs over, the one named last changes fastest.
Arguments:
- fields: float32 [4, 64, 32, 512], P(None, 'gz', 'gy'), may hold values from -4 to 4
- velocity: float32 [2, 64, 32, 512], P(None, 'gz', 'gy'), may hold values from -3 to 3
- face_rate: float32 [64, 32, 512], P('gz', 'gy'), may hold values from 1 to 4
- xy_rate: float32 [4], replicated, may hold values from 0.05 to 0.2
- z_scale: float32 [4], replicated, may hold values from 8 to 32
Outputs:
- advanced: float32 [4, 64, 32, 512], P(None, 'gz', 'gy')
The draws below stay inside these ranges and needn't reach their ends.
All inputs are finite; a program needn't handle non-finite values.
Results may differ from the reference program's by a relative error of at most 0.0003.
Values sent between devices are 32-bit elements; how exact they have to be, the bound alone decides.
A program may use at most 64 MiB of HBM per device.

```python
import math
import jax
import jax.numpy as jnp
from jax import lax

FIELDS = 4
STEPS = 2
NX = 512
NY = 32
NZ = 64


def draw_fields(key, part):
    shape = (FIELDS, NZ, NY, NX)
    column_shape = (FIELDS, 1, NY, NX)
    height = (jnp.arange(NZ, dtype=jnp.float32) + 0.5) / NZ
    rough = 0.8 * jax.random.normal(jax.random.fold_in(key, 5), shape, jnp.float32)
    contrast = 1.3 * jax.random.normal(jax.random.fold_in(key, 7), column_shape, jnp.float32)
    smooth = 0.5 + 1.5 * height
    values = rough + contrast + smooth[None, :, None, None]
    return jnp.clip(values, -4.0, 4.0)


def level_of(key, shape, shards, smallest, top_value):
    def one(dim, shards_of):
        steps = jax.random.uniform(jax.random.fold_in(jax.random.fold_in(key, 6), dim), (shards_of,), jnp.float32, smallest / len(shards), top_value / len(shards))
        return jnp.repeat(jnp.exp(steps), shape[dim] // shards_of).reshape((-1,) + (1,) * (len(shape) - dim - 1))

    gain = one(*shards[0])
    for cut in shards[1:]:
        gain = gain * one(*cut)
    return gain


def normal_values(stream_key, extent, deviation, most, shards=(), kind=jnp.bfloat16):
    factor_of = level_of(stream_key, extent, shards, -0.22, 0.18) if shards else 1.0
    values = jax.random.normal(stream_key, extent, jnp.float32) * deviation * factor_of
    return jnp.minimum(jnp.maximum(values, -most), most).astype(kind)


def setup_inputs(seed: int = 0) -> dict:
    seeds = jax.random.split(jax.random.key(seed), 6)
    fields = draw_fields(jax.random.fold_in(seeds[5], 71), 0)
    velocity = normal_values(seeds[1], (2, NZ, NY, NX), 0.5, 3.0, ((1, 16), (2, 2)), jnp.float32)
    face_rate = jnp.clip(jnp.exp(math.log(4.0) - 1.3862944 * jax.random.uniform(seeds[2], (NZ, NY, NX), jnp.float32) ** level_of(seeds[2], (NZ, NY, NX), ((0, 16), (1, 2)), -0.2, 0.2)), 1.0, 4.0)
    xy_rate = jnp.clip(jax.random.uniform(seeds[3], (FIELDS,), jnp.float32, 0.05, 0.2), 0.05, 0.2)
    z_scale = jnp.clip(jnp.exp(jax.random.uniform(seeds[4], (FIELDS,), jnp.float32, math.log(8.0), math.log(32.0))), 8.0, 32.0)
    return dict(fields=fields, velocity=velocity, face_rate=face_rate, xy_rate=xy_rate, z_scale=z_scale)


def tendency(present, along_x, along_y, spread):
    eastern = jnp.roll(present, -1, 2)
    western = jnp.roll(present, 1, 2)
    north = jnp.roll(present, -1, 1)
    south = jnp.roll(present, 1, 1)
    return spread * (eastern + western + north + south - 4.0 * present) - 0.5 * (along_x * (eastern - western) + along_y * (north - south))


def forward_sweep(carried, inputs):
    factor_prev, value_prev = carried
    source, face_below, face_above = inputs
    pivot = 1.0 + face_below + face_above + face_below * factor_prev
    factor_new = -face_above / pivot
    value_new = (source + face_below * value_prev) / pivot
    return (factor_new, value_new), (factor_new, value_new)


def backward_sweep(solved_above, inputs):
    factor_now, value_now = inputs
    solved = value_now - factor_now * solved_above
    return solved, solved


def advance_field(field_items, velocity, face_rate):
    present, spread, vertical_scale = field_items
    along_x = velocity[0]
    along_y = velocity[1]
    sectioned = present + tendency(present, along_x, along_y, spread)
    explicit = 0.5 * present + 0.5 * (sectioned + tendency(sectioned, along_x, along_y, spread))
    face_below = vertical_scale * face_rate
    face_above = jnp.concatenate([face_below[1:], jnp.zeros_like(face_below[:1])], 0)
    start = (jnp.zeros_like(present[0]), jnp.zeros_like(present[0]))
    ignored, sweeps = lax.scan(forward_sweep, start, (explicit, face_below, face_above))
    ignored, vertical = lax.scan(backward_sweep, jnp.zeros_like(present[0]), sweeps, reverse=True)
    return vertical


def reference(fields, velocity, face_rate, xy_rate, z_scale):
    def advance(field_items):
        return advance_field(field_items, velocity, face_rate)

    present = fields
    for step_index in range(STEPS):
        present = lax.map(advance, (present, xy_rate, z_scale))
    return present
```

```python
import functools

import jax
import jax.numpy as jnp
from jax import lax
from jax.experimental import pallas as pl
from jax.experimental.pallas import tpu as pltpu
from jax.sharding import PartitionSpec as P

STEPS = 2
TILE_ROWS = 8
TILE_LANES = 128
MESH = pl.DeviceIdType.MESH


def tendency(q, north, south, along_x, along_y, spread):
    width = q.shape[1]
    eastern = pltpu.roll(q, width - 1, 1)
    western = pltpu.roll(q, 1, 1)
    return spread * (eastern + western + north + south - 4.0 * q) - 0.5 * (
        along_x * (eastern - western) + along_y * (north - south)
    )


def join(lower, upper):
    between = lower[2] + upper[1]
    inverse = 1.0 / (lower[0] + upper[0] + between)
    to_low = lower[0] * inverse
    to_high = upper[0] * inverse
    element = (to_low * upper[0], lower[1] + to_low * between, upper[2] + to_high * between)
    return element, (to_low, to_high, inverse)


def layer_element(rate):
    return (rate, jnp.zeros_like(rate), jnp.ones_like(rate))


def kernel(
    plan,
    xy_rate,
    z_scale,
    fields,
    velocity,
    face_rate,
    out,
    present,
    speed,
    rates,
    rates_plane,
    coef0,
    held0,
    coef1,
    held1,
    coef2,
    send1,
    recv1,
    back1,
    home1,
    send2,
    recv2,
    back2,
    home2,
    send_el,
    recv_el,
    local_sem,
    halo_send,
    halo_recv,
    rate_send,
    rate_recv,
    s1_send,
    s1_recv,
    b1_send,
    b1_recv,
    s2_send,
    s2_recv,
    b2_send,
    b2_recv,
    el_send,
    el_recv,
):
    g1, g2, owners, per_field, fields_each, rows_each, gy_count = plan
    field_total, layers, rows, width = fields.shape
    halo = TILE_ROWS
    me = lax.axis_index("gz")
    my_y = lax.axis_index("gy")
    mine1 = lax.rem(me, g1)
    mine2 = lax.div(me, g1)
    upper_y = lax.rem(my_y + 1, gy_count)
    lower_y = lax.rem(my_y + gy_count - 1, gy_count)

    def plane_peer(offset):
        return lax.rem(mine1 + offset, g1)

    def plane_source(offset):
        return lax.rem(mine1 + g1 - offset, g1)

    def stack_peer(offset):
        return lax.rem(mine2 + offset, g2)

    def stack_source(offset):
        return lax.rem(mine2 + g2 - offset, g2)

    def plane_id(position):
        return {"gz": mine2 * g1 + position}

    def stack_id(position):
        return {"gz": position * g1 + mine1}

    def lanes(position):
        return pl.ds(pl.multiple_of(position * TILE_LANES, TILE_LANES), TILE_LANES)

    locals_in = [
        pltpu.make_async_copy(face_rate, rates, local_sem.at[0]),
        pltpu.make_async_copy(
            face_rate.at[:, :, lanes(mine1)], rates_plane.at[mine1], local_sem.at[1]
        ),
        pltpu.make_async_copy(fields, present.at[0, :, :, pl.ds(halo, rows)], local_sem.at[2]),
        pltpu.make_async_copy(velocity, speed.at[:, :, pl.ds(halo, rows)], local_sem.at[3]),
    ]
    for copy in locals_in:
        copy.start()

    barrier = pltpu.get_barrier_semaphore()
    for target in (lower_y, upper_y):
        pl.semaphore_signal(barrier, inc=1, device_id={"gy": target}, device_id_type=MESH)
    for offset in range(1, g1):
        pl.semaphore_signal(
            barrier, inc=1, device_id=plane_id(plane_peer(offset)), device_id_type=MESH
        )
    for offset in range(1, g2):
        pl.semaphore_signal(
            barrier, inc=1, device_id=stack_id(stack_peer(offset)), device_id_type=MESH
        )
    pl.semaphore_wait(barrier, 2 + g1 - 1 + g2 - 1)

    sent = []

    def remote(source, target, send_sem, recv_sem, device):
        copy = pltpu.make_async_remote_copy(
            src_ref=source,
            dst_ref=target,
            send_sem=send_sem,
            recv_sem=recv_sem,
            device_id=device,
            device_id_type=MESH,
        )
        return copy

    def halo_copies(source, first, target, slot):
        return [
            remote(
                source.at[:, :, pl.ds(first, halo)],
                target.at[:, :, pl.ds(halo + rows, halo)],
                halo_send.at[slot, 0],
                halo_recv.at[slot, 0],
                {"gy": lower_y},
            ),
            remote(
                source.at[:, :, pl.ds(first + rows - halo, halo)],
                target.at[:, :, pl.ds(0, halo)],
                halo_send.at[slot, 1],
                halo_recv.at[slot, 1],
                {"gy": upper_y},
            ),
        ]

    def begin(copies):
        for copy in copies:
            copy.start()
        sent.extend(copies)
        return copies

    halos = begin(halo_copies(fields, 0, present.at[0], 0))
    speed_halos = begin(halo_copies(velocity, 0, speed, STEPS))
    rate_copies = begin(
        [
            remote(
                face_rate.at[:, :, lanes(plane_peer(offset))],
                rates_plane.at[mine1],
                rate_send.at[offset - 1],
                rate_recv.at[offset - 1],
                plane_id(plane_peer(offset)),
            )
            for offset in range(1, g1)
        ]
    )

    locals_in[0].wait()

    def own_factors(f, carry):
        scale = z_scale[f]
        element = layer_element(scale * rates[0])
        for k in range(1, layers):
            element, factors = join(element, layer_element(scale * rates[k]))
            for n in range(3):
                coef0[n, k - 1, f] = factors[n]
        return carry

    lax.fori_loop(0, field_total, own_factors, 0)
    for copy in locals_in[1:]:
        copy.wait()

    def plane_factors():
        for copy in rate_copies:
            copy.wait_recv()

        def one(f, carry):
            scale = z_scale[f]
            total = None
            for i in range(g1):
                element = layer_element(scale * rates_plane[i, 0])
                for k in range(1, layers):
                    element, ignored = join(element, layer_element(scale * rates_plane[i, k]))
                if total is None:
                    total = element
                else:
                    total, factors = join(total, element)
                    for n in range(3):
                        coef1[n, i - 1, f] = factors[n]
            for n in range(3):
                for part in range(per_field):
                    cut = slice(part * rows_each, (part + 1) * rows_each)
                    send_el[f // fields_each * per_field + part, n, f % fields_each] = total[n][cut]
            return carry

        for f in range(field_total):
            one(f, 0)

    def to_owners(source, target, send_sem, recv_sem):
        copies = []
        for offset in range(1, g2):
            copies.append(
                remote(
                    source.at[lax.rem(stack_peer(offset), owners)],
                    target.at[mine2],
                    send_sem.at[offset - 1],
                    recv_sem.at[offset - 1],
                    stack_id(stack_peer(offset)),
                )
            )
        return copies

    def stack_factors():
        total = tuple(recv_el[0, n] for n in range(3))
        for g in range(1, g2):
            total, factors = join(total, tuple(recv_el[g, n] for n in range(3)))
            coef2[0, g - 1] = factors[1]
            coef2[1, g - 1] = factors[2]
        coef2[0, g2 - 1] = 1.0 / (total[0] + total[2])

    for step in range(STEPS):
        for copy in halos:
            copy.wait_recv()
        if step == 0:
            for copy in speed_halos:
                copy.wait_recv()

        def own_forward(f, carry):
            spread = xy_rate[f]
            low = None
            high = None
            inner = slice(halo, halo + rows)
            for k in range(layers):
                q = present[step, f, k]
                along_x = speed[0, k]
                along_y = speed[1, k]
                extent = q.shape[0]
                sectioned = q + tendency(
                    q, pltpu.roll(q, extent - 1, 0), pltpu.roll(q, 1, 0), along_x, along_y, spread
                )
                north = pltpu.roll(sectioned, extent - 1, 0)[inner]
                south = pltpu.roll(sectioned, 1, 0)[inner]
                middle = sectioned[inner]
                explicit = 0.5 * q[inner] + 0.5 * (
                    middle
                    + tendency(middle, north, south, along_x[inner], along_y[inner], spread)
                )
                if k == 0:
                    high = explicit
                else:
                    held0[k - 1, f] = high
                    share = coef0[0, k - 1, f] * high
                    low = share if low is None else low + share
                    high = explicit + coef0[1, k - 1, f] * high
            for c in range(g1):
                cut = slice(c * TILE_LANES, (c + 1) * TILE_LANES)
                send1[step, c, 0, f] = low[:, cut]
                send1[step, c, 1, f] = high[:, cut]
            return carry

        lax.fori_loop(0, field_total, own_forward, 0)

        out1 = begin(
            [
                remote(
                    send1.at[step, plane_peer(offset)],
                    recv1.at[step, mine1],
                    s1_send.at[step, offset - 1],
                    s1_recv.at[step, offset - 1],
                    plane_id(plane_peer(offset)),
                )
                for offset in range(1, g1)
            ]
        )
        recv1[step, mine1] = send1[step, mine1]
        if step == 0:
            plane_factors()
            elements = begin(to_owners(send_el, recv_el, el_send, el_recv))
            recv_el[mine2] = send_el[lax.rem(mine2, owners)]
        for copy in out1:
            copy.wait_recv()

        low = recv1[step, 0, 0]
        high = recv1[step, 0, 1]
        for i in range(1, g1):
            meeting = high + recv1[step, i, 0]
            held1[i - 1] = meeting
            low = low + coef1[0, i - 1] * meeting
            high = recv1[step, i, 1] + coef1[1, i - 1] * meeting
        for o in range(owners):
            field0 = o // per_field * fields_each
            row0 = o % per_field * rows_each
            cut = (slice(field0, field0 + fields_each), slice(row0, row0 + rows_each))
            send2[step, o, 0] = low[cut]
            send2[step, o, 1] = high[cut]
        out2 = begin(to_owners(send2.at[step], recv2.at[step], s2_send.at[step], s2_recv.at[step]))
        recv2[step, mine2] = send2[step, lax.rem(mine2, owners)]
        if step == 0:
            for copy in elements:
                copy.wait_recv()
            stack_factors()
        for copy in out2:
            copy.wait_recv()

        high = recv2[step, 0, 1]
        meetings = []
        for g in range(1, g2):
            meeting = high + recv2[step, g, 0]
            meetings.append(meeting)
            high = recv2[step, g, 1] + coef2[0, g - 1] * meeting
        value = high * coef2[0, g2 - 1]
        back2[step, g2 - 1, 1] = value
        for g in range(g2 - 1, 0, -1):
            value = meetings[g - 1] * coef2[1, g - 1] + coef2[0, g - 1] * value
            back2[step, g, 0] = value
            back2[step, g - 1, 1] = value
        back2[step, 0, 0] = jnp.zeros_like(value)
        home = []
        for offset in range(1, g2):
            home.append(
                remote(
                    back2.at[step, stack_peer(offset)],
                    home2.at[step, mine2],
                    b2_send.at[step, offset - 1],
                    b2_recv.at[step, offset - 1],
                    stack_id(stack_peer(offset)),
                )
            )
        begin(home)
        home2[step, mine2] = back2[step, mine2]
        for copy in home:
            copy.wait_recv()

        for o in range(owners):
            field0 = o // per_field * fields_each
            row0 = o % per_field * rows_each
            cut = (slice(field0, field0 + fields_each), slice(row0, row0 + rows_each))
            base = home2[step, o, 0]
            value = home2[step, o, 1]
            back1[(step, g1 - 1, 1) + cut] = value
            for i in range(g1 - 1, 0, -1):
                value = (
                    held1[(i - 1,) + cut] * coef1[(2, i - 1) + cut]
                    + coef1[(0, i - 1) + cut] * base
                    + coef1[(1, i - 1) + cut] * value
                )
                back1[(step, i, 0) + cut] = value
                back1[(step, i - 1, 1) + cut] = value
            back1[(step, 0, 0) + cut] = base
        home = begin(
            [
                remote(
                    back1.at[step, plane_peer(offset)],
                    home1.at[step, mine1],
                    b1_send.at[step, offset - 1],
                    b1_recv.at[step, offset - 1],
                    plane_id(plane_peer(offset)),
                )
                for offset in range(1, g1)
            ]
        )
        home1[step, mine1] = back1[step, mine1]
        for copy in home:
            copy.wait_recv()

        def own_backward(f, carry):
            for c in range(g1):
                cut = slice(c * TILE_LANES, (c + 1) * TILE_LANES)
                base = home1[step, c, 0, f]
                value = home1[step, c, 1, f]
                for k in range(layers - 1, -1, -1):
                    if k < layers - 1:
                        value = (
                            held0[k, f, :, cut] * coef0[2, k, f, :, cut]
                            + coef0[0, k, f, :, cut] * base
                            + coef0[1, k, f, :, cut] * value
                        )
                    if step == STEPS - 1:
                        out[f, k, :, cut] = value
                    else:
                        present[step + 1, f, k, halo : halo + rows, cut] = value
            return carry

        lax.fori_loop(0, field_total, own_backward, 0)
        if step < STEPS - 1:
            halos = begin(halo_copies(present.at[step + 1], halo, present.at[step + 1], step + 1))

    for copy in sent:
        copy.wait_send()


def on_device(fields, velocity, face_rate, xy_rate, z_scale):
    gz_count = lax.axis_size("gz")
    gy_count = lax.axis_size("gy")
    field_total, layers, rows, width = fields.shape
    g1 = width // TILE_LANES
    g2 = gz_count // g1
    owners = min(g2, field_total * rows // TILE_ROWS)
    per_field = max(1, owners // field_total)
    fields_each = max(1, field_total // owners)
    rows_each = rows // per_field
    plan = (g1, g2, owners, per_field, fields_each, rows_each, gy_count)
    extent = rows + 2 * TILE_ROWS
    share1 = (field_total, rows, TILE_LANES)
    share2 = (fields_each, rows_each, TILE_LANES)
    vmem = lambda *shape: pltpu.VMEM(shape, jnp.float32)
    dma = lambda *shape: pltpu.SemaphoreType.DMA(shape)
    return pl.pallas_call(
        functools.partial(kernel, plan),
        out_shape=jax.ShapeDtypeStruct(fields.shape, jnp.float32),
        in_specs=[pl.BlockSpec(memory_space=pltpu.SMEM)] * 2
        + [pl.BlockSpec(memory_space=pl.ANY)] * 3,
        out_specs=pl.BlockSpec(memory_space=pltpu.VMEM),
        scratch_shapes=[
            vmem(STEPS, field_total, layers, extent, width),
            vmem(2, layers, extent, width),
            vmem(layers, rows, width),
            vmem(g1, layers, rows, TILE_LANES),
            vmem(3, layers - 1, field_total, rows, width),
            vmem(layers - 1, field_total, rows, width),
            vmem(3, g1 - 1, *share1),
            vmem(g1 - 1, *share1),
            vmem(2, g2, *share2),
            vmem(STEPS, g1, 2, *share1),
            vmem(STEPS, g1, 2, *share1),
            vmem(STEPS, g1, 2, *share1),
            vmem(STEPS, g1, 2, *share1),
            vmem(STEPS, owners, 2, *share2),
            vmem(STEPS, g2, 2, *share2),
            vmem(STEPS, g2, 2, *share2),
            vmem(STEPS, g2, 2, *share2),
            vmem(owners, 3, *share2),
            vmem(g2, 3, *share2),
            dma(4),
            dma(STEPS + 1, 2),
            dma(STEPS + 1, 2),
            dma(g1 - 1),
            dma(g1 - 1),
            dma(STEPS, g1 - 1),
            dma(STEPS, g1 - 1),
            dma(STEPS, g1 - 1),
            dma(STEPS, g1 - 1),
            dma(STEPS, g2 - 1),
            dma(STEPS, g2 - 1),
            dma(STEPS, g2 - 1),
            dma(STEPS, g2 - 1),
            dma(g2 - 1),
            dma(g2 - 1),
        ],
        compiler_params=pltpu.CompilerParams(
            collective_id=0, has_side_effects=True, vmem_limit_bytes=40 * 1024 * 1024
        ),
        cost_estimate=pl.CostEstimate(
            flops=400 * fields.size, bytes_accessed=16 * fields.size, transcendentals=0
        ),
    )(xy_rate, z_scale, fields, velocity, face_rate)


def solution(mesh):
    in_specs = (P(None, "gz", "gy", None), P(None, "gz", "gy", None), P("gz", "gy", None), P(), P())
    out_specs = P(None, "gz", "gy", None)
    return jax.shard_map(
        on_device, mesh=mesh, in_specs=in_specs, out_specs=out_specs, check_vma=False
    )
```

```python
import functools

import jax
import jax.numpy as jnp
from jax import lax
from jax.experimental import pallas as pl
from jax.experimental.pallas import tpu as pltpu
from jax.sharding import PartitionSpec as P

STEPS = 2
TILE_ROWS = 8
TILE_LANES = 128
MESH = pl.DeviceIdType.MESH


def stencil(q, north, south, weights):
    width = q.shape[1]
    east, west, up, down, centre = weights
    eastern = pltpu.roll(q, width - 1, 1)
    western = pltpu.roll(q, 1, 1)
    return (east * eastern + west * western) + (up * north + down * south) + centre * q


def join(lower, upper):
    between = lower[2] + upper[1]
    inverse = 1.0 / (lower[0] + upper[0] + between)
    to_low = lower[0] * inverse
    to_high = upper[0] * inverse
    element = (to_low * upper[0], lower[1] + to_low * between, upper[2] + to_high * between)
    return element, (to_low, to_high, inverse)


def layer_element(rate):
    return (rate, jnp.zeros_like(rate), jnp.ones_like(rate))


def kernel(
    plan,
    xy_hbm,
    z_hbm,
    fields,
    velocity,
    face_rate,
    out,
    xy_rate,
    z_scale,
    present,
    speed,
    rates,
    rates_plane,
    coef0,
    held0,
    coef1,
    held1,
    coef2,
    send1,
    recv1,
    back1,
    home1,
    send2,
    recv2,
    back2,
    home2,
    send_el,
    recv_el,
    local_sem,
    field_sem,
    halo_send,
    halo_recv,
    speed_send,
    speed_recv,
    rate_send,
    rate_recv,
    s1_send,
    s1_recv,
    b1_send,
    b1_recv,
    s2_send,
    s2_recv,
    b2_send,
    b2_recv,
    el_send,
    el_recv,
):
    g1, g2, owners, per_field, fields_each, rows_each, gy_count = plan
    field_total, layers, rows, width = fields.shape
    halo = TILE_ROWS
    me = lax.axis_index("gz")
    my_y = lax.axis_index("gy")
    mine1 = lax.rem(me, g1)
    mine2 = lax.div(me, g1)
    upper_y = lax.rem(my_y + 1, gy_count)
    lower_y = lax.rem(my_y + gy_count - 1, gy_count)

    def plane_peer(offset):
        return lax.rem(mine1 + offset, g1)

    def stack_peer(offset):
        return lax.rem(mine2 + offset, g2)

    def plane_id(position):
        return {"gz": mine2 * g1 + position}

    def stack_id(position):
        return {"gz": position * g1 + mine1}

    def lanes(position):
        return pl.ds(pl.multiple_of(position * TILE_LANES, TILE_LANES), TILE_LANES)

    def each_field(body):
        def step_body(f, carry):
            body(f)
            return carry

        lax.fori_loop(0, field_total, step_body, 0)

    def remote(source, target, send_sem, recv_sem, device):
        return pltpu.make_async_remote_copy(
            src_ref=source,
            dst_ref=target,
            send_sem=send_sem,
            recv_sem=recv_sem,
            device_id=device,
            device_id_type=MESH,
        )

    def field_in(f):
        return pltpu.make_async_copy(
            fields.at[f], present.at[0, f, :, pl.ds(0, rows)], field_sem.at[f]
        )

    locals_in = [
        pltpu.make_async_copy(z_hbm, z_scale, local_sem.at[0]),
        pltpu.make_async_copy(xy_hbm, xy_rate, local_sem.at[1]),
        pltpu.make_async_copy(face_rate, rates, local_sem.at[2]),
        pltpu.make_async_copy(velocity, speed.at[:, :, pl.ds(0, rows)], local_sem.at[3]),
        pltpu.make_async_copy(
            face_rate.at[:, :, lanes(mine1)], rates_plane.at[mine1], local_sem.at[4]
        ),
    ]
    for copy in locals_in:
        copy.start()
    each_field(lambda f: field_in(f).start())

    barrier = pltpu.get_barrier_semaphore()
    for target in (lower_y, upper_y):
        pl.semaphore_signal(barrier, inc=1, device_id={"gy": target}, device_id_type=MESH)
    for offset in range(1, g1):
        pl.semaphore_signal(
            barrier, inc=1, device_id=plane_id(plane_peer(offset)), device_id_type=MESH
        )
    for offset in range(1, g2):
        pl.semaphore_signal(
            barrier, inc=1, device_id=stack_id(stack_peer(offset)), device_id_type=MESH
        )
    pl.semaphore_wait(barrier, 2 + g1 - 1 + g2 - 1)

    def halo_pair(source, target, send_sem, recv_sem):
        return [
            remote(
                source.at[..., pl.ds(0, halo), :],
                target.at[..., pl.ds(rows, halo), :],
                send_sem.at[0],
                recv_sem.at[0],
                {"gy": lower_y},
            ),
            remote(
                source.at[..., pl.ds(rows - halo, halo), :],
                target.at[..., pl.ds(rows + halo, halo), :],
                send_sem.at[1],
                recv_sem.at[1],
                {"gy": upper_y},
            ),
        ]

    def halos(step, f):
        source = fields.at[f] if step == 0 else present.at[step, f]
        return halo_pair(
            source, present.at[step, f], halo_send.at[step, f], halo_recv.at[step, f]
        )

    def rate_copy(offset):
        return remote(
            face_rate.at[:, :, lanes(plane_peer(offset))],
            rates_plane.at[mine1],
            rate_send.at[offset - 1],
            rate_recv.at[offset - 1],
            plane_id(plane_peer(offset)),
        )

    def out1(step, f, offset):
        return remote(
            send1.at[step, plane_peer(offset), f],
            recv1.at[step, mine1, f],
            s1_send.at[step, f, offset - 1],
            s1_recv.at[step, f, offset - 1],
            plane_id(plane_peer(offset)),
        )

    def in1(step, f, offset):
        return remote(
            back1.at[step, plane_peer(offset), f],
            home1.at[step, mine1, f],
            b1_send.at[step, f, offset - 1],
            b1_recv.at[step, f, offset - 1],
            plane_id(plane_peer(offset)),
        )

    def owner_of(f, part):
        return lax.div(f, fields_each) * per_field + part

    def out2(step, f, part):
        owner = owner_of(f, part)
        inner = lax.rem(f, fields_each)
        return remote(
            send2.at[step, f, part],
            recv2.at[step, inner, mine2],
            s2_send.at[step, f, part],
            s2_recv.at[step, inner, mine2],
            stack_id(owner),
        )

    def el_out(f, part):
        owner = owner_of(f, part)
        inner = lax.rem(f, fields_each)
        return remote(
            send_el.at[f, part],
            recv_el.at[inner, mine2],
            el_send.at[f, part],
            el_recv.at[inner, mine2],
            stack_id(owner),
        )

    def arrival2(buffer, source_of, recv_sem, inner, source):
        return remote(source_of, buffer.at[inner, source], recv_sem, recv_sem, stack_id(source))

    my_first = lax.div(mine2, per_field) * fields_each
    my_part = lax.rem(mine2, per_field)

    def in2(step, inner, offset):
        f = my_first + inner
        peer = stack_peer(offset)
        return remote(
            back2.at[step, inner, peer],
            home2.at[step, f, my_part],
            b2_send.at[step, inner, offset - 1],
            b2_recv.at[step, f, my_part],
            stack_id(peer),
        )

    def home_arrival(step, f, part):
        return remote(
            home2.at[step, f, part],
            home2.at[step, f, part],
            b2_recv.at[step, f, part],
            b2_recv.at[step, f, part],
            stack_id(owner_of(f, part)),
        )

    def as_owner(body):
        if owners == g2:
            body()
        else:
            pl.when(mine2 < owners)(body)

    def parts(f, same, other):
        for part in range(per_field):
            own = owner_of(f, part) == mine2
            if same is not None:
                pl.when(own)(functools.partial(same, part))
            pl.when(jnp.logical_not(own))(functools.partial(other, part))

    def rows_of(part):
        return slice(part * rows_each, (part + 1) * rows_each)

    speed_halos = halo_pair(velocity, speed, speed_send, speed_recv)
    for copy in speed_halos:
        copy.start()

    def start_halos(f):
        for copy in halos(0, f):
            copy.start()

    each_field(start_halos)
    for offset in range(1, g1):
        rate_copy(offset).start()

    for copy in locals_in[:3]:
        copy.wait()

    def own_factors(f):
        scale = z_scale[f]
        element = layer_element(scale * rates[0])
        for k in range(1, layers):
            element, factors = join(element, layer_element(scale * rates[k]))
            for n in range(3):
                coef0[n, k - 1, f] = factors[n]

    each_field(own_factors)

    def ring(block):
        place = lax.broadcasted_iota(jnp.int32, (halo, width), 0)
        edge = jnp.where(
            place < halo // 2, block[rows : rows + halo], block[rows + halo : rows + 2 * halo]
        )
        return jnp.concatenate([block[:rows], edge], axis=0)

    for copy in locals_in[3:]:
        copy.wait()
    for copy in speed_halos:
        copy.wait_recv()
    for n in range(2):
        for k in range(layers):
            speed[n, k, : rows + halo] = 0.5 * ring(speed[n, k])

    def plane_factors(f):
        scale = z_scale[f]
        total = None
        for i in range(g1):
            element = layer_element(scale * rates_plane[i, 0])
            for k in range(1, layers):
                element, ignored = join(element, layer_element(scale * rates_plane[i, k]))
            if total is None:
                total = element
            else:
                total, factors = join(total, element)
                for n in range(3):
                    coef1[n, i - 1, f] = factors[n]
        inner = lax.rem(f, fields_each)
        for part in range(per_field):
            for n in range(3):
                send_el[f, part, n] = total[n][rows_of(part)]

        def same(part):
            recv_el[inner, mine2] = send_el[f, part]

        parts(f, same, lambda part: el_out(f, part).start())

    def stack_factors():
        for inner in range(fields_each):
            for offset in range(1, g2):
                source = stack_peer(offset)
                arrival2(
                    recv_el, send_el.at[0, 0], el_recv.at[inner, source], inner, source
                ).wait_recv()
            total = tuple(recv_el[inner, 0, n] for n in range(3))
            for g in range(1, g2):
                total, factors = join(total, tuple(recv_el[inner, g, n] for n in range(3)))
                coef2[inner, 0, g - 1] = factors[1]
                coef2[inner, 1, g - 1] = factors[2]
            coef2[inner, 0, g2 - 1] = 1.0 / (total[0] + total[2])

    def own_forward(step, f):
        if step == 0:
            field_in(f).wait()
        for copy in halos(step, f):
            copy.wait_recv()
        spread = xy_rate[f]
        centre = 1.0 - 4.0 * spread
        low = None
        high = None
        extent = rows + halo
        for k in range(layers):
            q = ring(present[step, f, k])
            along_x = speed[0, k, :extent]
            along_y = speed[1, k, :extent]
            weights = (
                spread - along_x,
                spread + along_x,
                spread - along_y,
                spread + along_y,
                centre,
            )
            sectioned = stencil(q, pltpu.roll(q, extent - 1, 0), pltpu.roll(q, 1, 0), weights)
            north = pltpu.roll(sectioned, extent - 1, 0)[:rows]
            south = pltpu.roll(sectioned, 1, 0)[:rows]
            inner_weights = tuple(w[:rows] for w in weights[:4]) + (centre,)
            explicit = 0.5 * (
                q[:rows] + stencil(sectioned[:rows], north, south, inner_weights)
            )
            if k == 0:
                high = explicit
            else:
                held0[k - 1, f] = high
                share = coef0[0, k - 1, f] * high
                low = share if low is None else low + share
                high = explicit + coef0[1, k - 1, f] * high
        for c in range(g1):
            cut = slice(c * TILE_LANES, (c + 1) * TILE_LANES)
            send1[step, c, f, 0] = low[:, cut]
            send1[step, c, f, 1] = high[:, cut]
        for offset in range(1, g1):
            out1(step, f, offset).start()
        recv1[step, mine1, f] = send1[step, mine1, f]

    def plane_forward(step, f):
        for offset in range(1, g1):
            out1(step, f, offset).wait_recv()
        low = recv1[step, 0, f, 0]
        high = recv1[step, 0, f, 1]
        for i in range(1, g1):
            meeting = high + recv1[step, i, f, 0]
            held1[i - 1, f] = meeting
            low = low + coef1[0, i - 1, f] * meeting
            high = recv1[step, i, f, 1] + coef1[1, i - 1, f] * meeting
        for part in range(per_field):
            send2[step, f, part, 0] = low[rows_of(part)]
            send2[step, f, part, 1] = high[rows_of(part)]
        inner = lax.rem(f, fields_each)

        def same(part):
            recv2[step, inner, mine2] = send2[step, f, part]

        parts(f, same, lambda part: out2(step, f, part).start())

    def stack_solve(step):
        for inner in range(fields_each):
            for offset in range(1, g2):
                source = stack_peer(offset)
                arrival2(
                    recv2.at[step],
                    send2.at[step, 0, 0],
                    s2_recv.at[step, inner, source],
                    inner,
                    source,
                ).wait_recv()
            high = recv2[step, inner, 0, 1]
            meetings = []
            for g in range(1, g2):
                meeting = high + recv2[step, inner, g, 0]
                meetings.append(meeting)
                high = recv2[step, inner, g, 1] + coef2[inner, 0, g - 1] * meeting
            value = high * coef2[inner, 0, g2 - 1]
            back2[step, inner, g2 - 1, 1] = value
            for g in range(g2 - 1, 0, -1):
                value = (
                    meetings[g - 1] * coef2[inner, 1, g - 1] + coef2[inner, 0, g - 1] * value
                )
                back2[step, inner, g, 0] = value
                back2[step, inner, g - 1, 1] = value
            back2[step, inner, 0, 0] = jnp.zeros_like(value)
            for offset in range(1, g2):
                in2(step, inner, offset).start()
            home2[step, my_first + inner, my_part] = back2[step, inner, mine2]

    def plane_backward(step, f):
        parts(f, None, lambda part: home_arrival(step, f, part).wait_recv())
        for part in range(per_field):
            cut = rows_of(part)
            base = home2[step, f, part, 0]
            value = home2[step, f, part, 1]
            back1[step, g1 - 1, f, 1, cut] = value
            for i in range(g1 - 1, 0, -1):
                value = (
                    held1[i - 1, f, cut] * coef1[2, i - 1, f, cut]
                    + coef1[0, i - 1, f, cut] * base
                    + coef1[1, i - 1, f, cut] * value
                )
                back1[step, i, f, 0, cut] = value
                back1[step, i - 1, f, 1, cut] = value
            back1[step, 0, f, 0, cut] = base
        for offset in range(1, g1):
            in1(step, f, offset).start()
        home1[step, mine1, f] = back1[step, mine1, f]

    def own_backward(step, f):
        for offset in range(1, g1):
            in1(step, f, offset).wait_recv()
        for c in range(g1):
            cut = slice(c * TILE_LANES, (c + 1) * TILE_LANES)
            base = home1[step, c, f, 0]
            value = home1[step, c, f, 1]
            for k in range(layers - 1, -1, -1):
                if k < layers - 1:
                    value = (
                        held0[k, f, :, cut] * coef0[2, k, f, :, cut]
                        + coef0[0, k, f, :, cut] * base
                        + coef0[1, k, f, :, cut] * value
                    )
                if step == STEPS - 1:
                    out[f, k, :, cut] = value
                else:
                    present[step + 1, f, k, :rows, cut] = value
        if step < STEPS - 1:
            for copy in halos(step + 1, f):
                copy.start()

    for step in range(STEPS):
        each_field(functools.partial(own_forward, step))
        if step == 0:
            for offset in range(1, g1):
                rate_copy(offset).wait_recv()
            each_field(plane_factors)
        each_field(functools.partial(plane_forward, step))
        if step == 0:
            as_owner(stack_factors)
        as_owner(functools.partial(stack_solve, step))
        each_field(functools.partial(plane_backward, step))
        each_field(functools.partial(own_backward, step))

    for copy in speed_halos:
        copy.wait_send()
    for offset in range(1, g1):
        rate_copy(offset).wait_send()
    each_field(lambda f: parts(f, None, lambda part: el_out(f, part).wait_send()))
    for step in range(STEPS):

        def sent(f, step=step):
            for copy in halos(step, f):
                copy.wait_send()
            for offset in range(1, g1):
                out1(step, f, offset).wait_send()
                in1(step, f, offset).wait_send()
            parts(f, None, lambda part: out2(step, f, part).wait_send())

        def sent_back(step=step):
            for inner in range(fields_each):
                for offset in range(1, g2):
                    in2(step, inner, offset).wait_send()

        each_field(sent)
        as_owner(sent_back)


def on_device(fields, velocity, face_rate, xy_rate, z_scale):
    gz_count = lax.axis_size("gz")
    gy_count = lax.axis_size("gy")
    field_total, layers, rows, width = fields.shape
    g1 = width // TILE_LANES
    g2 = gz_count // g1
    owners = min(g2, field_total * rows // TILE_ROWS)
    per_field = max(1, owners // field_total)
    fields_each = max(1, field_total // owners)
    rows_each = rows // per_field
    plan = (g1, g2, owners, per_field, fields_each, rows_each, gy_count)
    extent = rows + 2 * TILE_ROWS
    share1 = (rows, TILE_LANES)
    share2 = (rows_each, TILE_LANES)
    vmem = lambda *shape: pltpu.VMEM(shape, jnp.float32)
    dma = lambda *shape: pltpu.SemaphoreType.DMA(shape)
    return pl.pallas_call(
        functools.partial(kernel, plan),
        out_shape=jax.ShapeDtypeStruct(fields.shape, jnp.float32),
        in_specs=[pl.BlockSpec(memory_space=pl.ANY)] * 5,
        out_specs=pl.BlockSpec(memory_space=pltpu.VMEM),
        scratch_shapes=[
            pltpu.SMEM((field_total,), jnp.float32),
            pltpu.SMEM((field_total,), jnp.float32),
            vmem(STEPS, field_total, layers, extent, width),
            vmem(2, layers, extent, width),
            vmem(layers, rows, width),
            vmem(g1, layers, rows, TILE_LANES),
            vmem(3, layers - 1, field_total, rows, width),
            vmem(layers - 1, field_total, rows, width),
            vmem(3, g1 - 1, field_total, *share1),
            vmem(g1 - 1, field_total, *share1),
            vmem(fields_each, 2, g2, *share2),
            vmem(STEPS, g1, field_total, 2, *share1),
            vmem(STEPS, g1, field_total, 2, *share1),
            vmem(STEPS, g1, field_total, 2, *share1),
            vmem(STEPS, g1, field_total, 2, *share1),
            vmem(STEPS, field_total, per_field, 2, *share2),
            vmem(STEPS, fields_each, g2, 2, *share2),
            vmem(STEPS, fields_each, g2, 2, *share2),
            vmem(STEPS, field_total, per_field, 2, *share2),
            vmem(field_total, per_field, 3, *share2),
            vmem(fields_each, g2, 3, *share2),
            dma(5),
            dma(field_total),
            dma(STEPS, field_total, 2),
            dma(STEPS, field_total, 2),
            dma(2),
            dma(2),
            dma(g1 - 1),
            dma(g1 - 1),
            dma(STEPS, field_total, g1 - 1),
            dma(STEPS, field_total, g1 - 1),
            dma(STEPS, field_total, g1 - 1),
            dma(STEPS, field_total, g1 - 1),
            dma(STEPS, field_total, per_field),
            dma(STEPS, fields_each, g2),
            dma(STEPS, fields_each, g2 - 1),
            dma(STEPS, field_total, per_field),
            dma(field_total, per_field),
            dma(fields_each, g2),
        ],
        compiler_params=pltpu.CompilerParams(
            collective_id=0, has_side_effects=True, vmem_limit_bytes=60 * 1024 * 1024
        ),
        cost_estimate=pl.CostEstimate(
            flops=400 * fields.size, bytes_accessed=16 * fields.size, transcendentals=0
        ),
    )(xy_rate, z_scale, fields, velocity, face_rate)


def solution(mesh):
    in_specs = (P(None, "gz", "gy", None), P(None, "gz", "gy", None), P("gz", "gy", None), P(), P())
    out_specs = P(None, "gz", "gy", None)
    return jax.shard_map(
        on_device, mesh=mesh, in_specs=in_specs, out_specs=out_specs, check_vma=False
    )
```

```python
import functools

import jax
import jax.numpy as jnp
from jax import lax
from jax.experimental import pallas as pl
from jax.experimental.pallas import tpu as pltpu
from jax.sharding import PartitionSpec as P

STEPS = 2
TILE_ROWS = 8
TILE_LANES = 128
MESH = pl.DeviceIdType.MESH


def stencil(q, north, south, weights):
    width = q.shape[1]
    east, west, up, down, centre = weights
    eastern = pltpu.roll(q, width - 1, 1)
    western = pltpu.roll(q, 1, 1)
    return (east * eastern + west * western) + (up * north + down * south) + centre * q


def join(lower, upper):
    between = lower[2] + upper[1]
    inverse = 1.0 / (lower[0] + upper[0] + between)
    to_low = lower[0] * inverse
    to_high = upper[0] * inverse
    element = (to_low * upper[0], lower[1] + to_low * between, upper[2] + to_high * between)
    return element, (to_low, to_high, inverse)


def layer_element(rate):
    return (rate, jnp.zeros_like(rate), jnp.ones_like(rate))


def kernel(
    plan,
    xy_hbm,
    z_hbm,
    fields,
    velocity,
    face_rate,
    out,
    xy_rate,
    z_scale,
    present,
    speed,
    rates,
    rates_plane,
    coef0,
    held0,
    coef1,
    held1,
    coef2,
    send1,
    recv1,
    back1,
    home1,
    send2,
    recv2,
    back2,
    home2,
    send_el,
    recv_el,
    local_sem,
    field_sem,
    halo_send,
    halo_recv,
    speed_send,
    speed_recv,
    rate_send,
    rate_recv,
    s1_send,
    s1_recv,
    b1_send,
    b1_recv,
    s2_send,
    s2_recv,
    b2_send,
    b2_recv,
    el_send,
    el_recv,
):
    g1, g2, owners, per_field, fields_each, rows_each, gy_count = plan
    field_total, layers, rows, width = fields.shape
    halo = TILE_ROWS
    me = lax.axis_index("gz")
    my_y = lax.axis_index("gy")
    mine1 = lax.rem(me, g1)
    mine2 = lax.div(me, g1)
    upper_y = lax.rem(my_y + 1, gy_count)
    lower_y = lax.rem(my_y + gy_count - 1, gy_count)

    def plane_peer(offset):
        return lax.rem(mine1 + offset, g1)

    def stack_peer(offset):
        return lax.rem(mine2 + offset, g2)

    def plane_id(position):
        return {"gz": mine2 * g1 + position}

    def stack_id(position):
        return {"gz": position * g1 + mine1}

    def lanes(position):
        return pl.ds(pl.multiple_of(position * TILE_LANES, TILE_LANES), TILE_LANES)

    def each_field(body):
        def step_body(f, carry):
            body(f)
            return carry

        lax.fori_loop(0, field_total, step_body, 0)

    def remote(source, target, send_sem, recv_sem, device):
        return pltpu.make_async_remote_copy(
            src_ref=source,
            dst_ref=target,
            send_sem=send_sem,
            recv_sem=recv_sem,
            device_id=device,
            device_id_type=MESH,
        )

    def await_bytes(ref, semaphore):
        pltpu.make_async_copy(ref, ref, semaphore).wait()

    def field_in(f):
        return pltpu.make_async_copy(
            fields.at[f], present.at[0, f, :, pl.ds(0, rows)], field_sem.at[f]
        )

    locals_in = [
        pltpu.make_async_copy(z_hbm, z_scale, local_sem.at[0]),
        pltpu.make_async_copy(xy_hbm, xy_rate, local_sem.at[1]),
        pltpu.make_async_copy(face_rate, rates, local_sem.at[2]),
        pltpu.make_async_copy(velocity, speed.at[:, :, pl.ds(0, rows)], local_sem.at[3]),
        pltpu.make_async_copy(
            face_rate.at[:, :, lanes(mine1)], rates_plane.at[mine1], local_sem.at[4]
        ),
    ]
    for copy in locals_in:
        copy.start()
    each_field(lambda f: field_in(f).start())

    barrier = pltpu.get_barrier_semaphore()
    for target in (lower_y, upper_y):
        pl.semaphore_signal(barrier, inc=1, device_id={"gy": target}, device_id_type=MESH)
    for offset in range(1, g1):
        pl.semaphore_signal(
            barrier, inc=1, device_id=plane_id(plane_peer(offset)), device_id_type=MESH
        )
    for offset in range(1, g2):
        pl.semaphore_signal(
            barrier, inc=1, device_id=stack_id(stack_peer(offset)), device_id_type=MESH
        )
    pl.semaphore_wait(barrier, 2 + g1 - 1 + g2 - 1)

    def halo_pair(source, target, send_sem, recv_sem):
        return [
            remote(
                source.at[..., pl.ds(0, halo), :],
                target.at[..., pl.ds(rows, halo), :],
                send_sem,
                recv_sem,
                {"gy": lower_y},
            ),
            remote(
                source.at[..., pl.ds(rows - halo, halo), :],
                target.at[..., pl.ds(rows + halo, halo), :],
                send_sem,
                recv_sem,
                {"gy": upper_y},
            ),
        ]

    def halos(step, f):
        source = fields.at[f] if step == 0 else present.at[step, f]
        return halo_pair(
            source, present.at[step, f], halo_send.at[step], halo_recv.at[step, f]
        )

    def rate_copy(offset):
        return remote(
            face_rate.at[:, :, lanes(plane_peer(offset))],
            rates_plane.at[mine1],
            rate_send.at[0],
            rate_recv.at[0],
            plane_id(plane_peer(offset)),
        )

    def out1(step, f, offset):
        return remote(
            send1.at[step, plane_peer(offset), f],
            recv1.at[step, mine1, f],
            s1_send.at[step],
            s1_recv.at[step, f],
            plane_id(plane_peer(offset)),
        )

    def in1(step, f, offset):
        return remote(
            back1.at[step, plane_peer(offset), f],
            home1.at[step, mine1, f],
            b1_send.at[step],
            b1_recv.at[step, f],
            plane_id(plane_peer(offset)),
        )

    def owner_of(f, part):
        return lax.div(f, fields_each) * per_field + part

    def out2(step, f, part):
        owner = owner_of(f, part)
        inner = lax.rem(f, fields_each)
        return remote(
            send2.at[step, f, part],
            recv2.at[step, inner, mine2],
            s2_send.at[step, f, part],
            s2_recv.at[step, inner],
            stack_id(owner),
        )

    def el_out(f, part):
        owner = owner_of(f, part)
        inner = lax.rem(f, fields_each)
        return remote(
            send_el.at[f, part],
            recv_el.at[inner, mine2],
            el_send.at[f, part],
            el_recv.at[inner],
            stack_id(owner),
        )

    my_first = lax.div(mine2, per_field) * fields_each
    my_part = lax.rem(mine2, per_field)

    def in2(step, inner, offset):
        f = my_first + inner
        peer = stack_peer(offset)
        return remote(
            back2.at[step, inner, peer],
            home2.at[step, f, my_part],
            b2_send.at[step, inner],
            b2_recv.at[step, f, my_part],
            stack_id(peer),
        )

    def as_owner(body):
        if owners == g2:
            body()
        else:
            pl.when(mine2 < owners)(body)

    def parts(f, same, other):
        for part in range(per_field):
            own = owner_of(f, part) == mine2
            if same is not None:
                pl.when(own)(functools.partial(same, part))
            pl.when(jnp.logical_not(own))(functools.partial(other, part))

    def rows_of(part):
        return slice(part * rows_each, (part + 1) * rows_each)

    speed_halos = halo_pair(velocity, speed, speed_send.at[0], speed_recv.at[0])
    for copy in speed_halos:
        copy.start()

    def start_halos(f):
        for copy in halos(0, f):
            copy.start()

    each_field(start_halos)
    for offset in range(1, g1):
        rate_copy(offset).start()

    for copy in locals_in[:3]:
        copy.wait()

    def own_factors(f):
        scale = z_scale[f]
        element = layer_element(scale * rates[0])
        for k in range(1, layers):
            element, factors = join(element, layer_element(scale * rates[k]))
            for n in range(3):
                coef0[n, k - 1, f] = factors[n]

    each_field(own_factors)

    def ring(block):
        place = lax.broadcasted_iota(jnp.int32, (halo, width), 0)
        edge = jnp.where(
            place < halo // 2, block[rows : rows + halo], block[rows + halo : rows + 2 * halo]
        )
        return jnp.concatenate([block[:rows], edge], axis=0)

    for copy in locals_in[3:]:
        copy.wait()
    await_bytes(speed.at[:, :, pl.ds(rows, 2 * halo)], speed_recv.at[0])
    for n in range(2):
        for k in range(layers):
            speed[n, k, : rows + halo] = 0.5 * ring(speed[n, k])

    def plane_factors(f):
        scale = z_scale[f]
        total = None
        for i in range(g1):
            element = layer_element(scale * rates_plane[i, 0])
            for k in range(1, layers):
                element, ignored = join(element, layer_element(scale * rates_plane[i, k]))
            if total is None:
                total = element
            else:
                total, factors = join(total, element)
                for n in range(3):
                    coef1[n, i - 1, f] = factors[n]
        inner = lax.rem(f, fields_each)
        for part in range(per_field):
            for n in range(3):
                send_el[f, part, n] = total[n][rows_of(part)]

        def same(part):
            recv_el[inner, mine2] = send_el[f, part]

        parts(f, same, lambda part: el_out(f, part).start())

    def stack_factors():
        for inner in range(fields_each):
            await_bytes(recv_el.at[inner, pl.ds(0, g2 - 1)], el_recv.at[inner])
            total = tuple(recv_el[inner, 0, n] for n in range(3))
            for g in range(1, g2):
                total, factors = join(total, tuple(recv_el[inner, g, n] for n in range(3)))
                coef2[inner, 0, g - 1] = factors[1]
                coef2[inner, 1, g - 1] = factors[2]
            coef2[inner, 0, g2 - 1] = 1.0 / (total[0] + total[2])

    def own_forward(step, f):
        if step == 0:
            field_in(f).wait()
        await_bytes(present.at[step, f, :, pl.ds(rows, 2 * halo)], halo_recv.at[step, f])
        spread = xy_rate[f]
        centre = 1.0 - 4.0 * spread
        low = None
        high = None
        extent = rows + halo
        for k in range(layers):
            q = ring(present[step, f, k])
            along_x = speed[0, k, :extent]
            along_y = speed[1, k, :extent]
            weights = (
                spread - along_x,
                spread + along_x,
                spread - along_y,
                spread + along_y,
                centre,
            )
            sectioned = stencil(q, pltpu.roll(q, extent - 1, 0), pltpu.roll(q, 1, 0), weights)
            north = pltpu.roll(sectioned, extent - 1, 0)[:rows]
            south = pltpu.roll(sectioned, 1, 0)[:rows]
            inner_weights = tuple(w[:rows] for w in weights[:4]) + (centre,)
            explicit = 0.5 * (
                q[:rows] + stencil(sectioned[:rows], north, south, inner_weights)
            )
            if k == 0:
                high = explicit
            else:
                held0[k - 1, f] = high
                share = coef0[0, k - 1, f] * high
                low = share if low is None else low + share
                high = explicit + coef0[1, k - 1, f] * high
        for c in range(g1):
            cut = slice(c * TILE_LANES, (c + 1) * TILE_LANES)
            send1[step, c, f, 0] = low[:, cut]
            send1[step, c, f, 1] = high[:, cut]
        for offset in range(1, g1):
            out1(step, f, offset).start()
        recv1[step, mine1, f] = send1[step, mine1, f]

    def plane_forward(step, f):
        await_bytes(recv1.at[step, pl.ds(0, g1 - 1), f], s1_recv.at[step, f])
        low = recv1[step, 0, f, 0]
        high = recv1[step, 0, f, 1]
        for i in range(1, g1):
            meeting = high + recv1[step, i, f, 0]
            held1[i - 1, f] = meeting
            low = low + coef1[0, i - 1, f] * meeting
            high = recv1[step, i, f, 1] + coef1[1, i - 1, f] * meeting
        for part in range(per_field):
            send2[step, f, part, 0] = low[rows_of(part)]
            send2[step, f, part, 1] = high[rows_of(part)]
        inner = lax.rem(f, fields_each)

        def same(part):
            recv2[step, inner, mine2] = send2[step, f, part]

        parts(f, same, lambda part: out2(step, f, part).start())

    def stack_solve(step):
        for inner in range(fields_each):
            await_bytes(recv2.at[step, inner, pl.ds(0, g2 - 1)], s2_recv.at[step, inner])
            high = recv2[step, inner, 0, 1]
            meetings = []
            for g in range(1, g2):
                meeting = high + recv2[step, inner, g, 0]
                meetings.append(meeting)
                high = recv2[step, inner, g, 1] + coef2[inner, 0, g - 1] * meeting
            value = high * coef2[inner, 0, g2 - 1]
            back2[step, inner, g2 - 1, 1] = value
            for g in range(g2 - 1, 0, -1):
                value = (
                    meetings[g - 1] * coef2[inner, 1, g - 1] + coef2[inner, 0, g - 1] * value
                )
                back2[step, inner, g, 0] = value
                back2[step, inner, g - 1, 1] = value
            back2[step, inner, 0, 0] = jnp.zeros_like(value)
            for offset in range(1, g2):
                in2(step, inner, offset).start()
            home2[step, my_first + inner, my_part] = back2[step, inner, mine2]

    def plane_backward(step, f):
        parts(
            f, None, lambda part: await_bytes(home2.at[step, f, part], b2_recv.at[step, f, part])
        )
        for part in range(per_field):
            cut = rows_of(part)
            base = home2[step, f, part, 0]
            value = home2[step, f, part, 1]
            back1[step, g1 - 1, f, 1, cut] = value
            for i in range(g1 - 1, 0, -1):
                value = (
                    held1[i - 1, f, cut] * coef1[2, i - 1, f, cut]
                    + coef1[0, i - 1, f, cut] * base
                    + coef1[1, i - 1, f, cut] * value
                )
                back1[step, i, f, 0, cut] = value
                back1[step, i - 1, f, 1, cut] = value
            back1[step, 0, f, 0, cut] = base
        for offset in range(1, g1):
            in1(step, f, offset).start()
        home1[step, mine1, f] = back1[step, mine1, f]

    def own_backward(step, f):
        await_bytes(home1.at[step, pl.ds(0, g1 - 1), f], b1_recv.at[step, f])
        for c in range(g1):
            cut = slice(c * TILE_LANES, (c + 1) * TILE_LANES)
            base = home1[step, c, f, 0]
            value = home1[step, c, f, 1]
            for k in range(layers - 1, -1, -1):
                if k < layers - 1:
                    value = (
                        held0[k, f, :, cut] * coef0[2, k, f, :, cut]
                        + coef0[0, k, f, :, cut] * base
                        + coef0[1, k, f, :, cut] * value
                    )
                if step == STEPS - 1:
                    out[f, k, :, cut] = value
                else:
                    present[step + 1, f, k, :rows, cut] = value
        if step < STEPS - 1:
            for copy in halos(step + 1, f):
                copy.start()

    def sent_out(step):
        await_bytes(present.at[step, :, :, pl.ds(rows, 2 * halo)], halo_send.at[step])
        await_bytes(send1.at[step, pl.ds(0, g1 - 1)], s1_send.at[step])
        each_field(lambda f: parts(f, None, lambda part: out2(step, f, part).wait_send()))

    def sent_home(step):
        def stack():
            for inner in range(fields_each):
                await_bytes(back2.at[step, inner, pl.ds(0, g2 - 1)], b2_send.at[step, inner])

        as_owner(stack)
        await_bytes(back1.at[step, pl.ds(0, g1 - 1)], b1_send.at[step])

    each_field(functools.partial(own_forward, 0))
    await_bytes(rates_plane.at[pl.ds(0, g1 - 1)], rate_recv.at[0])
    each_field(plane_factors)
    for step in range(STEPS):
        each_field(functools.partial(plane_forward, step))
        if step == 0:
            as_owner(stack_factors)
        as_owner(functools.partial(stack_solve, step))
        each_field(functools.partial(plane_backward, step))
        if step == 0:
            await_bytes(speed.at[:, :, pl.ds(rows, 2 * halo)], speed_send.at[0])
            await_bytes(rates_plane.at[pl.ds(0, g1 - 1)], rate_send.at[0])
            each_field(lambda f: parts(f, None, lambda part: el_out(f, part).wait_send()))
        sent_out(step)
        if step < STEPS - 1:
            own_backward(step, 0)

            def turn(f, carry, step=step):
                own_backward(step, f)
                own_forward(step + 1, f - 1)
                return carry

            lax.fori_loop(1, field_total, turn, 0)
            own_forward(step + 1, field_total - 1)
            sent_home(step)
        else:
            each_field(functools.partial(own_backward, step))
            sent_home(step)


def on_device(fields, velocity, face_rate, xy_rate, z_scale):
    gz_count = lax.axis_size("gz")
    gy_count = lax.axis_size("gy")
    field_total, layers, rows, width = fields.shape
    g1 = width // TILE_LANES
    g2 = gz_count // g1
    owners = min(g2, field_total * rows // TILE_ROWS)
    per_field = max(1, owners // field_total)
    fields_each = max(1, field_total // owners)
    rows_each = rows // per_field
    plan = (g1, g2, owners, per_field, fields_each, rows_each, gy_count)
    extent = rows + 2 * TILE_ROWS
    share1 = (rows, TILE_LANES)
    share2 = (rows_each, TILE_LANES)
    vmem = lambda *shape: pltpu.VMEM(shape, jnp.float32)
    dma = lambda *shape: pltpu.SemaphoreType.DMA(shape)
    return pl.pallas_call(
        functools.partial(kernel, plan),
        out_shape=jax.ShapeDtypeStruct(fields.shape, jnp.float32),
        in_specs=[pl.BlockSpec(memory_space=pl.ANY)] * 5,
        out_specs=pl.BlockSpec(memory_space=pltpu.VMEM),
        scratch_shapes=[
            pltpu.SMEM((field_total,), jnp.float32),
            pltpu.SMEM((field_total,), jnp.float32),
            vmem(STEPS, field_total, layers, extent, width),
            vmem(2, layers, extent, width),
            vmem(layers, rows, width),
            vmem(g1, layers, rows, TILE_LANES),
            vmem(3, layers - 1, field_total, rows, width),
            vmem(layers - 1, field_total, rows, width),
            vmem(3, g1 - 1, field_total, *share1),
            vmem(g1 - 1, field_total, *share1),
            vmem(fields_each, 2, g2, *share2),
            vmem(STEPS, g1, field_total, 2, *share1),
            vmem(STEPS, g1, field_total, 2, *share1),
            vmem(STEPS, g1, field_total, 2, *share1),
            vmem(STEPS, g1, field_total, 2, *share1),
            vmem(STEPS, field_total, per_field, 2, *share2),
            vmem(STEPS, fields_each, g2, 2, *share2),
            vmem(STEPS, fields_each, g2, 2, *share2),
            vmem(STEPS, field_total, per_field, 2, *share2),
            vmem(field_total, per_field, 3, *share2),
            vmem(fields_each, g2, 3, *share2),
            dma(5),
            dma(field_total),
            dma(STEPS),
            dma(STEPS, field_total),
            dma(1),
            dma(1),
            dma(1),
            dma(1),
            dma(STEPS),
            dma(STEPS, field_total),
            dma(STEPS),
            dma(STEPS, field_total),
            dma(STEPS, field_total, per_field),
            dma(STEPS, fields_each),
            dma(STEPS, fields_each),
            dma(STEPS, field_total, per_field),
            dma(field_total, per_field),
            dma(fields_each),
        ],
        compiler_params=pltpu.CompilerParams(
            collective_id=0, has_side_effects=True, vmem_limit_bytes=60 * 1024 * 1024
        ),
        cost_estimate=pl.CostEstimate(
            flops=400 * fields.size, bytes_accessed=16 * fields.size, transcendentals=0
        ),
    )(xy_rate, z_scale, fields, velocity, face_rate)


def solution(mesh):
    in_specs = (P(None, "gz", "gy", None), P(None, "gz", "gy", None), P("gz", "gy", None), P(), P())
    out_specs = P(None, "gz", "gy", None)
    return jax.shard_map(
        on_device, mesh=mesh, in_specs=in_specs, out_specs=out_specs, check_vma=False
    )
```

```python
import functools

import jax
import jax.numpy as jnp
from jax import lax
from jax.experimental import pallas as pl
from jax.experimental.pallas import tpu as pltpu
from jax.sharding import PartitionSpec as P

STEPS = 2
TILE_ROWS = 8
TILE_LANES = 128
MESH = pl.DeviceIdType.MESH


def stencil(q, north, south, weights):
    width = q.shape[1]
    east, west, up, down, centre = weights
    eastern = pltpu.roll(q, width - 1, 1)
    western = pltpu.roll(q, 1, 1)
    return (east * eastern + west * western) + (up * north + down * south) + centre * q


def join(lower, upper):
    between = lower[2] + upper[1]
    inverse = 1.0 / (lower[0] + upper[0] + between)
    to_low = lower[0] * inverse
    to_high = upper[0] * inverse
    element = (to_low * upper[0], lower[1] + to_low * between, upper[2] + to_high * between)
    return element, (to_low, to_high, inverse)


def layer_element(rate):
    return (rate, jnp.zeros_like(rate), jnp.ones_like(rate))


def kernel(
    plan,
    xy_hbm,
    z_hbm,
    fields,
    velocity,
    face_rate,
    out,
    xy_rate,
    z_scale,
    present,
    speed,
    rates,
    rates_plane,
    coef0,
    held0,
    coef1,
    held1,
    coef2,
    held2,
    send1,
    recv1,
    back1,
    home1,
    send2,
    recv2,
    send_el,
    recv_el,
    local_sem,
    field_sem,
    halo_send,
    halo_recv,
    speed_send,
    speed_recv,
    rate_send,
    rate_recv,
    s1_send,
    s1_recv,
    b1_send,
    b1_recv,
    s2_send,
    s2_recv,
    el_send,
    el_recv,
):
    g1, g2, rounds, gy_count = plan
    field_total, layers, rows, width = fields.shape
    halo = TILE_ROWS
    me = lax.axis_index("gz")
    my_y = lax.axis_index("gy")
    mine1 = lax.rem(me, g1)
    mine2 = lax.div(me, g1)
    upper_y = lax.rem(my_y + 1, gy_count)
    lower_y = lax.rem(my_y + gy_count - 1, gy_count)

    def plane_peer(offset):
        return lax.rem(mine1 + offset, g1)

    def stack_bit(t):
        return lax.rem(lax.div(mine2, 2**t), 2)

    def stack_peer(t):
        return mine2 + (1 - 2 * stack_bit(t)) * 2**t

    def pick(t, lower, upper):
        return jnp.where(jnp.broadcast_to(stack_bit(t), lower.shape) == 0, lower, upper)

    def plane_id(position):
        return {"gz": mine2 * g1 + position}

    def stack_id(position):
        return {"gz": position * g1 + mine1}

    def lanes(position):
        return pl.ds(pl.multiple_of(position * TILE_LANES, TILE_LANES), TILE_LANES)

    def each_field(body):
        def step_body(f, carry):
            body(f)
            return carry

        lax.fori_loop(0, field_total, step_body, 0)

    def remote(source, target, send_sem, recv_sem, device):
        return pltpu.make_async_remote_copy(
            src_ref=source,
            dst_ref=target,
            send_sem=send_sem,
            recv_sem=recv_sem,
            device_id=device,
            device_id_type=MESH,
        )

    def await_bytes(ref, semaphore):
        pltpu.make_async_copy(ref, ref, semaphore).wait()

    def field_in(f):
        return pltpu.make_async_copy(
            fields.at[f], present.at[0, f, :, pl.ds(0, rows)], field_sem.at[f]
        )

    locals_in = [
        pltpu.make_async_copy(z_hbm, z_scale, local_sem.at[0]),
        pltpu.make_async_copy(xy_hbm, xy_rate, local_sem.at[1]),
        pltpu.make_async_copy(face_rate, rates, local_sem.at[2]),
        pltpu.make_async_copy(velocity, speed.at[:, :, pl.ds(0, rows)], local_sem.at[3]),
        pltpu.make_async_copy(
            face_rate.at[:, :, lanes(mine1)], rates_plane.at[mine1], local_sem.at[4]
        ),
    ]
    for copy in locals_in:
        copy.start()
    each_field(lambda f: field_in(f).start())

    barrier = pltpu.get_barrier_semaphore()
    for target in (lower_y, upper_y):
        pl.semaphore_signal(barrier, inc=1, device_id={"gy": target}, device_id_type=MESH)
    for offset in range(1, g1):
        pl.semaphore_signal(
            barrier, inc=1, device_id=plane_id(plane_peer(offset)), device_id_type=MESH
        )
    for t in range(rounds):
        pl.semaphore_signal(
            barrier, inc=1, device_id=stack_id(stack_peer(t)), device_id_type=MESH
        )
    pl.semaphore_wait(barrier, 2 + g1 - 1 + rounds)

    def halo_pair(source, target, send_sem, recv_sem):
        return [
            remote(
                source.at[..., pl.ds(0, halo), :],
                target.at[..., pl.ds(rows, halo), :],
                send_sem,
                recv_sem,
                {"gy": lower_y},
            ),
            remote(
                source.at[..., pl.ds(rows - halo, halo), :],
                target.at[..., pl.ds(rows + halo, halo), :],
                send_sem,
                recv_sem,
                {"gy": upper_y},
            ),
        ]

    def halos(step, f):
        source = fields.at[f] if step == 0 else present.at[step, f]
        return halo_pair(
            source, present.at[step, f], halo_send.at[step], halo_recv.at[step, f]
        )

    def rate_copy(offset):
        return remote(
            face_rate.at[:, :, lanes(plane_peer(offset))],
            rates_plane.at[mine1],
            rate_send.at[0],
            rate_recv.at[0],
            plane_id(plane_peer(offset)),
        )

    def out1(step, f, offset):
        return remote(
            send1.at[step, plane_peer(offset), f],
            recv1.at[step, mine1, f],
            s1_send.at[step],
            s1_recv.at[step, f],
            plane_id(plane_peer(offset)),
        )

    def in1(step, f, offset):
        return remote(
            back1.at[step, plane_peer(offset), f],
            home1.at[step, mine1, f],
            b1_send.at[step],
            b1_recv.at[step, f],
            plane_id(plane_peer(offset)),
        )

    last = rounds - 1

    def payload2(buffer, step, t, f):
        return buffer.at[step, t, f, pl.ds(0, 1 if t == last else 2)]

    def payload_el(buffer, t, f):
        return buffer.at[t, f, pl.ds(0, 1 if t == last else 3)]

    def pair2(step, t, f):
        return remote(
            payload2(send2, step, t, f),
            payload2(recv2, step, t, f),
            s2_send.at[step, t],
            s2_recv.at[step, t, f],
            stack_id(stack_peer(t)),
        )

    def pair_el(t, f):
        return remote(
            payload_el(send_el, t, f),
            payload_el(recv_el, t, f),
            el_send.at[t],
            el_recv.at[t, f],
            stack_id(stack_peer(t)),
        )

    speed_halos = halo_pair(velocity, speed, speed_send.at[0], speed_recv.at[0])
    for copy in speed_halos:
        copy.start()

    def start_halos(f):
        for copy in halos(0, f):
            copy.start()

    each_field(start_halos)
    for offset in range(1, g1):
        rate_copy(offset).start()

    for copy in locals_in[:3]:
        copy.wait()

    def own_factors(f):
        scale = z_scale[f]
        element = layer_element(scale * rates[0])
        for k in range(1, layers):
            element, factors = join(element, layer_element(scale * rates[k]))
            for n in range(3):
                coef0[n, k - 1, f] = factors[n]

    each_field(own_factors)

    def ring(block):
        place = lax.broadcasted_iota(jnp.int32, (halo, width), 0)
        edge = jnp.where(
            place < halo // 2, block[rows : rows + halo], block[rows + halo : rows + 2 * halo]
        )
        return jnp.concatenate([block[:rows], edge], axis=0)

    for copy in locals_in[3:]:
        copy.wait()
    await_bytes(speed.at[:, :, pl.ds(rows, 2 * halo)], speed_recv.at[0])
    for n in range(2):
        for k in range(layers):
            speed[n, k, : rows + halo] = 0.5 * ring(speed[n, k])

    def plane_factors(f):
        scale = z_scale[f]
        total = None
        for i in range(g1):
            element = layer_element(scale * rates_plane[i, 0])
            for k in range(1, layers):
                element, ignored = join(element, layer_element(scale * rates_plane[i, k]))
            if total is None:
                total = element
            else:
                total, factors = join(total, element)
                for n in range(3):
                    coef1[n, i - 1, f] = factors[n]
        offer_element(0, f, total)

    def offer_element(t, f, element):
        if t < last:
            for n in range(3):
                send_el[t, f, n] = element[n]
        else:
            closing = element[0] + element[2]
            inverse = 1.0 / closing
            ratio = element[0] * inverse
            coef2[0, t, f] = ratio
            coef2[1, t, f] = inverse
            send_el[t, f, 0] = pick(t, closing, element[1] + ratio * element[2])
        pair_el(t, f).start()

    def stack_factors(t, f):
        await_bytes(payload_el(recv_el, t, f), el_recv.at[t, f])
        if t < last:
            mine = tuple(send_el[t, f, n] for n in range(3))
            other = tuple(recv_el[t, f, n] for n in range(3))
            lower = tuple(pick(t, a, b) for a, b in zip(mine, other))
            upper = tuple(pick(t, b, a) for a, b in zip(mine, other))
            total, factors = join(lower, upper)
            for n in range(3):
                coef2[n, t, f] = factors[n]
            offer_element(t + 1, f, total)
        else:
            coef2[2, t, f] = 1.0 / (send_el[t, f, 0] + recv_el[t, f, 0])

    def own_forward(step, f):
        if step == 0:
            field_in(f).wait()
        await_bytes(present.at[step, f, :, pl.ds(rows, 2 * halo)], halo_recv.at[step, f])
        spread = xy_rate[f]
        centre = 1.0 - 4.0 * spread
        low = None
        high = None
        extent = rows + halo
        for k in range(layers):
            q = ring(present[step, f, k])
            along_x = speed[0, k, :extent]
            along_y = speed[1, k, :extent]
            weights = (
                spread - along_x,
                spread + along_x,
                spread - along_y,
                spread + along_y,
                centre,
            )
            sectioned = stencil(q, pltpu.roll(q, extent - 1, 0), pltpu.roll(q, 1, 0), weights)
            north = pltpu.roll(sectioned, extent - 1, 0)[:rows]
            south = pltpu.roll(sectioned, 1, 0)[:rows]
            inner_weights = tuple(w[:rows] for w in weights[:4]) + (centre,)
            explicit = 0.5 * (
                q[:rows] + stencil(sectioned[:rows], north, south, inner_weights)
            )
            if k == 0:
                high = explicit
            else:
                held0[k - 1, f] = high
                share = coef0[0, k - 1, f] * high
                low = share if low is None else low + share
                high = explicit + coef0[1, k - 1, f] * high
        for c in range(g1):
            cut = slice(c * TILE_LANES, (c + 1) * TILE_LANES)
            send1[step, c, f, 0] = low[:, cut]
            send1[step, c, f, 1] = high[:, cut]
        for offset in range(1, g1):
            out1(step, f, offset).start()
        recv1[step, mine1, f] = send1[step, mine1, f]

    def plane_forward(step, f):
        await_bytes(recv1.at[step, pl.ds(0, g1 - 1), f], s1_recv.at[step, f])
        low = recv1[step, 0, f, 0]
        high = recv1[step, 0, f, 1]
        for i in range(1, g1):
            meeting = high + recv1[step, i, f, 0]
            held1[i - 1, f] = meeting
            low = low + coef1[0, i - 1, f] * meeting
            high = recv1[step, i, f, 1] + coef1[1, i - 1, f] * meeting
        offer(step, 0, f, low, high)

    def offer(step, t, f, low, high):
        if t < last:
            send2[step, t, f, 0] = low
        else:
            send2[step, t, f, 0] = pick(t, high, low + coef2[0, t, f] * high)
        send2[step, t, f, 1] = high
        pair2(step, t, f).start()

    def stack_round(step, t, f):
        await_bytes(payload2(recv2, step, t, f), s2_recv.at[step, t, f])
        low = send2[step, t, f, 0]
        high = send2[step, t, f, 1]
        other_low = recv2[step, t, f, 0]
        if t < last:
            other_high = recv2[step, t, f, 1]
            meeting = pick(t, high, other_high) + pick(t, other_low, low)
            held2[t, f] = meeting
            low, high = (
                pick(t, low, other_low) + coef2[0, t, f] * meeting,
                pick(t, other_high, high) + coef2[1, t, f] * meeting,
            )
            offer(step, t + 1, f, low, high)
            return
        middle = (low + other_low) * coef2[2, t, f]
        top = high * coef2[1, t, f] + coef2[0, t, f] * middle
        base = pick(t, jnp.zeros_like(middle), middle)
        value = pick(t, middle, top)
        for r in range(last - 1, -1, -1):
            middle = (
                held2[r, f] * coef2[2, r, f] + coef2[0, r, f] * base + coef2[1, r, f] * value
            )
            base, value = pick(r, base, middle), pick(r, middle, value)
        back1[step, g1 - 1, f, 1] = value
        for i in range(g1 - 1, 0, -1):
            value = (
                held1[i - 1, f] * coef1[2, i - 1, f]
                + coef1[0, i - 1, f] * base
                + coef1[1, i - 1, f] * value
            )
            back1[step, i, f, 0] = value
            back1[step, i - 1, f, 1] = value
        back1[step, 0, f, 0] = base
        for offset in range(1, g1):
            in1(step, f, offset).start()
        home1[step, mine1, f] = back1[step, mine1, f]

    def own_backward(step, f):
        await_bytes(home1.at[step, pl.ds(0, g1 - 1), f], b1_recv.at[step, f])
        for c in range(g1):
            cut = slice(c * TILE_LANES, (c + 1) * TILE_LANES)
            base = home1[step, c, f, 0]
            value = home1[step, c, f, 1]
            for k in range(layers - 1, -1, -1):
                if k < layers - 1:
                    value = (
                        held0[k, f, :, cut] * coef0[2, k, f, :, cut]
                        + coef0[0, k, f, :, cut] * base
                        + coef0[1, k, f, :, cut] * value
                    )
                if step == STEPS - 1:
                    out[f, k, :, cut] = value
                else:
                    present[step + 1, f, k, :rows, cut] = value
        if step < STEPS - 1:
            for copy in halos(step + 1, f):
                copy.start()

    def sent_out(step):
        await_bytes(present.at[step, :, :, pl.ds(rows, 2 * halo)], halo_send.at[step])
        await_bytes(send1.at[step, pl.ds(0, g1 - 1)], s1_send.at[step])
        for t in range(rounds):
            await_bytes(send2.at[step, t, :, pl.ds(0, 1 if t == last else 2)], s2_send.at[step, t])

    def sent_home(step):
        await_bytes(back1.at[step, pl.ds(0, g1 - 1)], b1_send.at[step])

    each_field(functools.partial(own_forward, 0))
    await_bytes(rates_plane.at[pl.ds(0, g1 - 1)], rate_recv.at[0])
    each_field(plane_factors)
    for step in range(STEPS):
        each_field(functools.partial(plane_forward, step))
        for t in range(rounds):
            if step == 0:
                each_field(functools.partial(stack_factors, t))
            each_field(functools.partial(stack_round, step, t))
        if step == 0:
            await_bytes(speed.at[:, :, pl.ds(rows, 2 * halo)], speed_send.at[0])
            await_bytes(rates_plane.at[pl.ds(0, g1 - 1)], rate_send.at[0])
            for t in range(rounds):
                await_bytes(send_el.at[t, :, pl.ds(0, 1 if t == last else 3)], el_send.at[t])
        sent_out(step)
        if step < STEPS - 1:
            own_backward(step, 0)

            def turn(f, carry, step=step):
                own_backward(step, f)
                own_forward(step + 1, f - 1)
                return carry

            lax.fori_loop(1, field_total, turn, 0)
            own_forward(step + 1, field_total - 1)
            sent_home(step)
        else:
            each_field(functools.partial(own_backward, step))
            sent_home(step)


def on_device(fields, velocity, face_rate, xy_rate, z_scale):
    gz_count = lax.axis_size("gz")
    gy_count = lax.axis_size("gy")
    field_total, layers, rows, width = fields.shape
    g1 = width // TILE_LANES
    g2 = gz_count // g1
    rounds = g2.bit_length() - 1
    assert g1 * 2**rounds == gz_count
    plan = (g1, g2, rounds, gy_count)
    extent = rows + 2 * TILE_ROWS
    share1 = (rows, TILE_LANES)
    vmem = lambda *shape: pltpu.VMEM(shape, jnp.float32)
    dma = lambda *shape: pltpu.SemaphoreType.DMA(shape)
    return pl.pallas_call(
        functools.partial(kernel, plan),
        out_shape=jax.ShapeDtypeStruct(fields.shape, jnp.float32),
        in_specs=[pl.BlockSpec(memory_space=pl.ANY)] * 5,
        out_specs=pl.BlockSpec(memory_space=pltpu.VMEM),
        scratch_shapes=[
            pltpu.SMEM((field_total,), jnp.float32),
            pltpu.SMEM((field_total,), jnp.float32),
            vmem(STEPS, field_total, layers, extent, width),
            vmem(2, layers, extent, width),
            vmem(layers, rows, width),
            vmem(g1, layers, rows, TILE_LANES),
            vmem(3, layers - 1, field_total, rows, width),
            vmem(layers - 1, field_total, rows, width),
            vmem(3, g1 - 1, field_total, *share1),
            vmem(g1 - 1, field_total, *share1),
            vmem(3, rounds, field_total, *share1),
            vmem(rounds, field_total, *share1),
            vmem(STEPS, g1, field_total, 2, *share1),
            vmem(STEPS, g1, field_total, 2, *share1),
            vmem(STEPS, g1, field_total, 2, *share1),
            vmem(STEPS, g1, field_total, 2, *share1),
            vmem(STEPS, rounds, field_total, 2, *share1),
            vmem(STEPS, rounds, field_total, 2, *share1),
            vmem(rounds, field_total, 3, *share1),
            vmem(rounds, field_total, 3, *share1),
            dma(5),
            dma(field_total),
            dma(STEPS),
            dma(STEPS, field_total),
            dma(1),
            dma(1),
            dma(1),
            dma(1),
            dma(STEPS),
            dma(STEPS, field_total),
            dma(STEPS),
            dma(STEPS, field_total),
            dma(STEPS, rounds),
            dma(STEPS, rounds, field_total),
            dma(rounds),
            dma(rounds, field_total),
        ],
        compiler_params=pltpu.CompilerParams(
            collective_id=0, has_side_effects=True, vmem_limit_bytes=60 * 1024 * 1024
        ),
        cost_estimate=pl.CostEstimate(
            flops=400 * fields.size, bytes_accessed=16 * fields.size, transcendentals=0
        ),
    )(xy_rate, z_scale, fields, velocity, face_rate)


def solution(mesh):
    in_specs = (P(None, "gz", "gy", None), P(None, "gz", "gy", None), P("gz", "gy", None), P(), P())
    out_specs = P(None, "gz", "gy", None)
    return jax.shard_map(
        on_device, mesh=mesh, in_specs=in_specs, out_specs=out_specs, check_vma=False
    )
```

```python
import functools

import jax
import jax.numpy as jnp
from jax import lax
from jax.experimental import pallas as pl
from jax.experimental.pallas import tpu as pltpu
from jax.sharding import PartitionSpec as P

STEPS = 2
TILE_ROWS = 8
TILE_LANES = 128
MESH = pl.DeviceIdType.MESH


def stencil(q, north, south, weights):
    width = q.shape[1]
    east, west, up, down, centre = weights
    eastern = pltpu.roll(q, width - 1, 1)
    western = pltpu.roll(q, 1, 1)
    return (east * eastern + west * western) + (up * north + down * south) + centre * q


def join(lower, upper):
    between = lower[2] + upper[1]
    inverse = 1.0 / (lower[0] + upper[0] + between)
    to_low = lower[0] * inverse
    to_high = upper[0] * inverse
    element = (to_low * upper[0], lower[1] + to_low * between, upper[2] + to_high * between)
    return element, (to_low, to_high, inverse)


def layer_element(rate):
    return (rate, jnp.zeros_like(rate), jnp.ones_like(rate))


def kernel(
    plan,
    xy_hbm,
    z_hbm,
    fields,
    velocity,
    face_rate,
    out,
    xy_rate,
    z_scale,
    present,
    speed,
    rates,
    rates_plane,
    coef0,
    held0,
    coef1,
    held1,
    coef2,
    held2,
    send1,
    recv1,
    back1,
    home1,
    send2,
    recv2,
    send_el,
    recv_el,
    local_sem,
    field_sem,
    halo_send,
    halo_recv,
    speed_send,
    speed_recv,
    rate_send,
    rate_recv,
    s1_send,
    s1_recv,
    b1_send,
    b1_recv,
    s2_send,
    s2_recv,
    el_send,
    el_recv,
):
    g1, g2, rounds, gy_count = plan
    field_total, layers, rows, width = fields.shape
    halo = TILE_ROWS
    me = lax.axis_index("gz")
    my_y = lax.axis_index("gy")
    mine1 = lax.rem(me, g1)
    mine2 = lax.div(me, g1)
    upper_y = lax.rem(my_y + 1, gy_count)
    lower_y = lax.rem(my_y + gy_count - 1, gy_count)

    def plane_peer(offset):
        return lax.rem(mine1 + offset, g1)

    def stack_bit(t):
        return lax.rem(lax.div(mine2, 2**t), 2)

    def stack_peer(t):
        return mine2 + (1 - 2 * stack_bit(t)) * 2**t

    def pick(t, lower, upper):
        return jnp.where(jnp.broadcast_to(stack_bit(t), lower.shape) == 0, lower, upper)

    def plane_id(position):
        return {"gz": mine2 * g1 + position}

    def stack_id(position):
        return {"gz": position * g1 + mine1}

    def lanes(position):
        return pl.ds(pl.multiple_of(position * TILE_LANES, TILE_LANES), TILE_LANES)

    def each_field(body):
        def step_body(f, carry):
            body(f)
            return carry

        lax.fori_loop(0, field_total, step_body, 0)

    def remote(source, target, send_sem, recv_sem, device):
        return pltpu.make_async_remote_copy(
            src_ref=source,
            dst_ref=target,
            send_sem=send_sem,
            recv_sem=recv_sem,
            device_id=device,
            device_id_type=MESH,
        )

    def await_bytes(ref, semaphore):
        pltpu.make_async_copy(ref, ref, semaphore).wait()

    def field_in(f):
        return pltpu.make_async_copy(
            fields.at[f], present.at[0, f, :, pl.ds(0, rows)], field_sem.at[f]
        )

    locals_in = [
        pltpu.make_async_copy(z_hbm, z_scale, local_sem.at[0]),
        pltpu.make_async_copy(xy_hbm, xy_rate, local_sem.at[1]),
        pltpu.make_async_copy(face_rate, rates, local_sem.at[2]),
        pltpu.make_async_copy(velocity, speed.at[:, :, pl.ds(0, rows)], local_sem.at[3]),
        pltpu.make_async_copy(
            face_rate.at[:, :, lanes(mine1)], rates_plane.at[mine1], local_sem.at[4]
        ),
    ]
    for copy in locals_in:
        copy.start()
    each_field(lambda f: field_in(f).start())

    barrier = pltpu.get_barrier_semaphore()
    for target in (lower_y, upper_y):
        pl.semaphore_signal(barrier, inc=1, device_id={"gy": target}, device_id_type=MESH)
    for offset in range(1, g1):
        pl.semaphore_signal(
            barrier, inc=1, device_id=plane_id(plane_peer(offset)), device_id_type=MESH
        )
    for t in range(rounds):
        pl.semaphore_signal(
            barrier, inc=1, device_id=stack_id(stack_peer(t)), device_id_type=MESH
        )
    pl.semaphore_wait(barrier, 2 + g1 - 1 + rounds)

    def halo_pair(source, target, send_sem, recv_sem):
        return [
            remote(
                source.at[..., pl.ds(0, halo), :],
                target.at[..., pl.ds(rows, halo), :],
                send_sem,
                recv_sem,
                {"gy": lower_y},
            ),
            remote(
                source.at[..., pl.ds(rows - halo, halo), :],
                target.at[..., pl.ds(rows + halo, halo), :],
                send_sem,
                recv_sem,
                {"gy": upper_y},
            ),
        ]

    def halos(step, f):
        source = fields.at[f] if step == 0 else present.at[step, f]
        return halo_pair(
            source, present.at[step, f], halo_send.at[step], halo_recv.at[step, f]
        )

    def rate_copy(offset):
        return remote(
            face_rate.at[:, :, lanes(plane_peer(offset))],
            rates_plane.at[mine1],
            rate_send.at[0],
            rate_recv.at[0],
            plane_id(plane_peer(offset)),
        )

    def out1(step, f, offset):
        return remote(
            send1.at[step, plane_peer(offset), f],
            recv1.at[step, mine1, f],
            s1_send.at[step],
            s1_recv.at[step, f],
            plane_id(plane_peer(offset)),
        )

    def in1(step, f, offset):
        return remote(
            back1.at[step, plane_peer(offset), f],
            home1.at[step, mine1, f],
            b1_send.at[step],
            b1_recv.at[step, f],
            plane_id(plane_peer(offset)),
        )

    last = rounds - 1

    def payload2(buffer, step, t, f):
        return buffer.at[step, t, f, pl.ds(0, 1 if t == last else 2)]

    def payload_el(buffer, t, f):
        return buffer.at[t, f, pl.ds(0, 1 if t == last else 3)]

    def pair2(step, t, f):
        return remote(
            payload2(send2, step, t, f),
            payload2(recv2, step, t, f),
            s2_send.at[step, t],
            s2_recv.at[step, t, f],
            stack_id(stack_peer(t)),
        )

    def pair_el(t, f):
        return remote(
            payload_el(send_el, t, f),
            payload_el(recv_el, t, f),
            el_send.at[t],
            el_recv.at[t, f],
            stack_id(stack_peer(t)),
        )

    speed_halos = halo_pair(velocity, speed, speed_send.at[0], speed_recv.at[0])
    for copy in speed_halos:
        copy.start()

    def start_halos(f):
        for copy in halos(0, f):
            copy.start()

    each_field(start_halos)
    for offset in range(1, g1):
        rate_copy(offset).start()

    for copy in locals_in[:3]:
        copy.wait()

    def own_factors(f):
        scale = z_scale[f]
        element = layer_element(scale * rates[0])
        for k in range(1, layers):
            element, factors = join(element, layer_element(scale * rates[k]))
            for n in range(3):
                coef0[n, k - 1, f] = factors[n]

    each_field(own_factors)

    def ring(block):
        place = lax.broadcasted_iota(jnp.int32, (halo, width), 0)
        edge = jnp.where(
            place < halo // 2, block[rows : rows + halo], block[rows + halo : rows + 2 * halo]
        )
        return jnp.concatenate([block[:rows], edge], axis=0)

    locals_in[3].wait()
    await_bytes(speed.at[:, :, pl.ds(rows, 2 * halo)], speed_recv.at[0])
    for n in range(2):
        for k in range(layers):
            speed[n, k, : rows + halo] = 0.5 * ring(speed[n, k])

    def plane_factors(f):
        scale = z_scale[f]
        total = None
        for i in range(g1):
            element = layer_element(scale * rates_plane[i, 0])
            for k in range(1, layers):
                element, ignored = join(element, layer_element(scale * rates_plane[i, k]))
            if total is None:
                total = element
            else:
                total, factors = join(total, element)
                for n in range(3):
                    coef1[n, i - 1, f] = factors[n]
        offer_element(0, f, total)

    def offer_element(t, f, element):
        if t < last:
            for n in range(3):
                send_el[t, f, n] = element[n]
        else:
            closing = element[0] + element[2]
            inverse = 1.0 / closing
            ratio = element[0] * inverse
            coef2[0, t, f] = ratio
            coef2[1, t, f] = inverse
            send_el[t, f, 0] = pick(t, closing, element[1] + ratio * element[2])
        pair_el(t, f).start()

    def stack_factors(t, f):
        await_bytes(payload_el(recv_el, t, f), el_recv.at[t, f])
        if t < last:
            mine = tuple(send_el[t, f, n] for n in range(3))
            other = tuple(recv_el[t, f, n] for n in range(3))
            lower = tuple(pick(t, a, b) for a, b in zip(mine, other))
            upper = tuple(pick(t, b, a) for a, b in zip(mine, other))
            total, factors = join(lower, upper)
            for n in range(3):
                coef2[n, t, f] = factors[n]
            offer_element(t + 1, f, total)
        else:
            coef2[2, t, f] = 1.0 / (send_el[t, f, 0] + recv_el[t, f, 0])

    def own_forward(step, f):
        if step == 0:
            field_in(f).wait()
        await_bytes(present.at[step, f, :, pl.ds(rows, 2 * halo)], halo_recv.at[step, f])
        spread = xy_rate[f]
        centre = 1.0 - 4.0 * spread
        low = None
        high = None
        extent = rows + halo
        for k in range(layers):
            q = ring(present[step, f, k])
            along_x = speed[0, k, :extent]
            along_y = speed[1, k, :extent]
            weights = (
                spread - along_x,
                spread + along_x,
                spread - along_y,
                spread + along_y,
                centre,
            )
            sectioned = stencil(q, pltpu.roll(q, extent - 1, 0), pltpu.roll(q, 1, 0), weights)
            north = pltpu.roll(sectioned, extent - 1, 0)[:rows]
            south = pltpu.roll(sectioned, 1, 0)[:rows]
            inner_weights = tuple(w[:rows] for w in weights[:4]) + (centre,)
            explicit = q[:rows] + stencil(sectioned[:rows], north, south, inner_weights)
            if step < STEPS - 1:
                explicit = 0.5 * explicit
            if k == 0:
                high = explicit
            else:
                held0[k - 1, f] = high
                share = coef0[0, k - 1, f] * high
                low = share if low is None else low + share
                high = explicit + coef0[1, k - 1, f] * high
        for c in range(g1):
            cut = slice(c * TILE_LANES, (c + 1) * TILE_LANES)
            send1[step, c, f, 0] = low[:, cut]
            send1[step, c, f, 1] = high[:, cut]
        for offset in range(1, g1):
            out1(step, f, offset).start()
        recv1[step, mine1, f] = send1[step, mine1, f]

    def plane_forward(step, f):
        await_bytes(recv1.at[step, pl.ds(0, g1 - 1), f], s1_recv.at[step, f])
        low = recv1[step, 0, f, 0]
        high = recv1[step, 0, f, 1]
        for i in range(1, g1):
            meeting = high + recv1[step, i, f, 0]
            held1[i - 1, f] = meeting
            low = low + coef1[0, i - 1, f] * meeting
            high = recv1[step, i, f, 1] + coef1[1, i - 1, f] * meeting
        offer(step, 0, f, low, high)

    def offer(step, t, f, low, high):
        if t < last:
            send2[step, t, f, 0] = low
        else:
            send2[step, t, f, 0] = pick(t, high, low + coef2[0, t, f] * high)
        send2[step, t, f, 1] = high
        pair2(step, t, f).start()

    def stack_round(step, t, f):
        await_bytes(payload2(recv2, step, t, f), s2_recv.at[step, t, f])
        low = send2[step, t, f, 0]
        high = send2[step, t, f, 1]
        other_low = recv2[step, t, f, 0]
        if t < last:
            other_high = recv2[step, t, f, 1]
            meeting = pick(t, high, other_high) + pick(t, other_low, low)
            held2[t, f] = meeting
            low, high = (
                pick(t, low, other_low) + coef2[0, t, f] * meeting,
                pick(t, other_high, high) + coef2[1, t, f] * meeting,
            )
            offer(step, t + 1, f, low, high)
            return
        middle = (low + other_low) * coef2[2, t, f]
        top = high * coef2[1, t, f] + coef2[0, t, f] * middle
        base = pick(t, jnp.zeros_like(middle), middle)
        value = pick(t, middle, top)
        for r in range(last - 1, -1, -1):
            middle = (
                held2[r, f] * coef2[2, r, f] + coef2[0, r, f] * base + coef2[1, r, f] * value
            )
            base, value = pick(r, base, middle), pick(r, middle, value)
        back1[step, g1 - 1, f, 1] = value
        for i in range(g1 - 1, 0, -1):
            value = (
                held1[i - 1, f] * coef1[2, i - 1, f]
                + coef1[0, i - 1, f] * base
                + coef1[1, i - 1, f] * value
            )
            back1[step, i, f, 0] = value
            back1[step, i - 1, f, 1] = value
        back1[step, 0, f, 0] = base
        for offset in range(1, g1):
            in1(step, f, offset).start()
        home1[step, mine1, f] = back1[step, mine1, f]

    def own_backward(step, f):
        await_bytes(home1.at[step, pl.ds(0, g1 - 1), f], b1_recv.at[step, f])
        for c in range(g1):
            cut = slice(c * TILE_LANES, (c + 1) * TILE_LANES)
            base = home1[step, c, f, 0]
            value = home1[step, c, f, 1]
            for k in range(layers - 1, -1, -1):
                if k < layers - 1:
                    value = (
                        held0[k, f, :, cut] * coef0[2, k, f, :, cut]
                        + coef0[0, k, f, :, cut] * base
                        + coef0[1, k, f, :, cut] * value
                    )
                if step == STEPS - 1:
                    out[f, k, :, cut] = value
                else:
                    present[step + 1, f, k, :rows, cut] = value
        if step < STEPS - 1:
            for copy in halos(step + 1, f):
                copy.start()

    def sent_out(step):
        await_bytes(present.at[step, :, :, pl.ds(rows, 2 * halo)], halo_send.at[step])
        await_bytes(send1.at[step, pl.ds(0, g1 - 1)], s1_send.at[step])
        for t in range(rounds):
            await_bytes(send2.at[step, t, :, pl.ds(0, 1 if t == last else 2)], s2_send.at[step, t])

    def sent_home(step):
        await_bytes(back1.at[step, pl.ds(0, g1 - 1)], b1_send.at[step])

    def opening(f):
        own_forward(0, f)

        @pl.when(f == 0)
        def plane():
            locals_in[4].wait()
            await_bytes(rates_plane.at[pl.ds(0, g1 - 1)], rate_recv.at[0])
            each_field(plane_factors)

        for t in range(rounds):

            @pl.when(f == min(t + 2, field_total - 1))
            def stack(t=t):
                each_field(functools.partial(stack_factors, t))

    each_field(opening)
    for step in range(STEPS):
        each_field(functools.partial(plane_forward, step))
        for t in range(rounds):
            each_field(functools.partial(stack_round, step, t))
        if step == 0:
            await_bytes(speed.at[:, :, pl.ds(rows, 2 * halo)], speed_send.at[0])
            await_bytes(rates_plane.at[pl.ds(0, g1 - 1)], rate_send.at[0])
            for t in range(rounds):
                await_bytes(send_el.at[t, :, pl.ds(0, 1 if t == last else 3)], el_send.at[t])
        sent_out(step)
        if step < STEPS - 1:
            own_backward(step, 0)

            def turn(f, carry, step=step):
                own_backward(step, f)
                own_forward(step + 1, f - 1)
                return carry

            lax.fori_loop(1, field_total, turn, 0)
            own_forward(step + 1, field_total - 1)
            sent_home(step)
        else:
            each_field(functools.partial(own_backward, step))
            sent_home(step)


def on_device(fields, velocity, face_rate, xy_rate, z_scale):
    gz_count = lax.axis_size("gz")
    gy_count = lax.axis_size("gy")
    field_total, layers, rows, width = fields.shape
    g1 = width // TILE_LANES
    g2 = gz_count // g1
    rounds = g2.bit_length() - 1
    assert g1 * 2**rounds == gz_count
    plan = (g1, g2, rounds, gy_count)
    extent = rows + 2 * TILE_ROWS
    share1 = (rows, TILE_LANES)
    vmem = lambda *shape: pltpu.VMEM(shape, jnp.float32)
    dma = lambda *shape: pltpu.SemaphoreType.DMA(shape)
    doubled = pl.pallas_call(
        functools.partial(kernel, plan),
        out_shape=jax.ShapeDtypeStruct(fields.shape, jnp.float32),
        in_specs=[pl.BlockSpec(memory_space=pl.ANY)] * 5,
        out_specs=pl.BlockSpec(memory_space=pltpu.VMEM),
        scratch_shapes=[
            pltpu.SMEM((field_total,), jnp.float32),
            pltpu.SMEM((field_total,), jnp.float32),
            vmem(STEPS, field_total, layers, extent, width),
            vmem(2, layers, extent, width),
            vmem(layers, rows, width),
            vmem(g1, layers, rows, TILE_LANES),
            vmem(3, layers - 1, field_total, rows, width),
            vmem(layers - 1, field_total, rows, width),
            vmem(3, g1 - 1, field_total, *share1),
            vmem(g1 - 1, field_total, *share1),
            vmem(3, rounds, field_total, *share1),
            vmem(rounds, field_total, *share1),
            vmem(STEPS, g1, field_total, 2, *share1),
            vmem(STEPS, g1, field_total, 2, *share1),
            vmem(STEPS, g1, field_total, 2, *share1),
            vmem(STEPS, g1, field_total, 2, *share1),
            vmem(STEPS, rounds, field_total, 2, *share1),
            vmem(STEPS, rounds, field_total, 2, *share1),
            vmem(rounds, field_total, 3, *share1),
            vmem(rounds, field_total, 3, *share1),
            dma(5),
            dma(field_total),
            dma(STEPS),
            dma(STEPS, field_total),
            dma(1),
            dma(1),
            dma(1),
            dma(1),
            dma(STEPS),
            dma(STEPS, field_total),
            dma(STEPS),
            dma(STEPS, field_total),
            dma(STEPS, rounds),
            dma(STEPS, rounds, field_total),
            dma(rounds),
            dma(rounds, field_total),
        ],
        compiler_params=pltpu.CompilerParams(
            collective_id=0, has_side_effects=True, vmem_limit_bytes=60 * 1024 * 1024
        ),
        cost_estimate=pl.CostEstimate(
            flops=400 * fields.size, bytes_accessed=16 * fields.size, transcendentals=0
        ),
    )(xy_rate, z_scale, fields, velocity, face_rate)
    return 0.5 * doubled


def solution(mesh):
    in_specs = (P(None, "gz", "gy", None), P(None, "gz", "gy", None), P("gz", "gy", None), P(), P())
    out_specs = P(None, "gz", "gy", None)
    return jax.shard_map(
        on_device, mesh=mesh, in_specs=in_specs, out_specs=out_specs, check_vma=False
    )
```

```python
import functools

import jax
import jax.numpy as jnp
from jax import lax
from jax.experimental import pallas as pl
from jax.experimental.pallas import tpu as pltpu
from jax.sharding import PartitionSpec as P

STEPS = 2
TILE_ROWS = 8
TILE_LANES = 128
MESH = pl.DeviceIdType.MESH


def stencil(q, north, south, weights):
    width = q.shape[1]
    east, west, up, down, centre = weights
    eastern = pltpu.roll(q, width - 1, 1)
    western = pltpu.roll(q, 1, 1)
    return (east * eastern + west * western) + (up * north + down * south) + centre * q


def reciprocal(value):
    estimate = pl.reciprocal(value, approx=True)
    estimate = estimate * (2.0 - value * estimate)
    return estimate * (2.0 - value * estimate)


def join(lower, upper):
    between = lower[2] + upper[1]
    inverse = reciprocal(lower[0] + upper[0] + between)
    to_low = lower[0] * inverse
    to_high = upper[0] * inverse
    element = (to_low * upper[0], lower[1] + to_low * between, upper[2] + to_high * between)
    return element, (to_low, to_high, inverse)


def layer_element(rate):
    return (rate, jnp.zeros_like(rate), jnp.ones_like(rate))


def kernel(
    plan,
    xy_hbm,
    z_hbm,
    fields,
    velocity,
    face_rate,
    out,
    xy_rate,
    z_scale,
    present,
    speed,
    rates,
    rates_plane,
    coef0,
    held0,
    coef1,
    held1,
    coef2,
    held2,
    result,
    send1,
    recv1,
    back1,
    home1,
    send2,
    recv2,
    send_el,
    recv_el,
    local_sem,
    field_sem,
    out_sem,
    halo_send,
    halo_recv,
    speed_send,
    speed_recv,
    rate_send,
    rate_recv,
    s1_send,
    s1_recv,
    b1_send,
    b1_recv,
    s2_send,
    s2_recv,
    el_send,
    el_recv,
):
    g1, g2, rounds, gy_count = plan
    field_total, layers, rows, width = fields.shape
    halo = TILE_ROWS
    me = lax.axis_index("gz")
    my_y = lax.axis_index("gy")
    mine1 = lax.rem(me, g1)
    mine2 = lax.div(me, g1)
    upper_y = lax.rem(my_y + 1, gy_count)
    lower_y = lax.rem(my_y + gy_count - 1, gy_count)

    def plane_peer(offset):
        return lax.rem(mine1 + offset, g1)

    def stack_bit(t):
        return lax.rem(lax.div(mine2, 2**t), 2)

    def stack_peer(t):
        return mine2 + (1 - 2 * stack_bit(t)) * 2**t

    def pick(t, lower, upper):
        return jnp.where(jnp.broadcast_to(stack_bit(t), lower.shape) == 0, lower, upper)

    def plane_id(position):
        return {"gz": mine2 * g1 + position}

    def stack_id(position):
        return {"gz": position * g1 + mine1}

    def lanes(position):
        return pl.ds(pl.multiple_of(position * TILE_LANES, TILE_LANES), TILE_LANES)

    def each_field(body):
        def step_body(f, carry):
            body(f)
            return carry

        lax.fori_loop(0, field_total, step_body, 0)

    def remote(source, target, send_sem, recv_sem, device):
        return pltpu.make_async_remote_copy(
            src_ref=source,
            dst_ref=target,
            send_sem=send_sem,
            recv_sem=recv_sem,
            device_id=device,
            device_id_type=MESH,
        )

    def await_bytes(ref, semaphore):
        pltpu.make_async_copy(ref, ref, semaphore).wait()

    def field_in(f):
        return pltpu.make_async_copy(
            fields.at[f], present.at[0, f, :, pl.ds(0, rows)], field_sem.at[f]
        )

    def field_out(f):
        return pltpu.make_async_copy(result.at[f], out.at[f], out_sem.at[f])

    locals_in = [
        pltpu.make_async_copy(z_hbm, z_scale, local_sem.at[0]),
        pltpu.make_async_copy(xy_hbm, xy_rate, local_sem.at[1]),
        pltpu.make_async_copy(face_rate, rates, local_sem.at[2]),
        pltpu.make_async_copy(velocity, speed.at[:, :, pl.ds(0, rows)], local_sem.at[3]),
        pltpu.make_async_copy(
            face_rate.at[:, :, lanes(mine1)], rates_plane.at[mine1], local_sem.at[4]
        ),
    ]
    for copy in locals_in:
        copy.start()
    each_field(lambda f: field_in(f).start())

    barrier = pltpu.get_barrier_semaphore()
    for target in (lower_y, upper_y):
        pl.semaphore_signal(barrier, inc=1, device_id={"gy": target}, device_id_type=MESH)
    for offset in range(1, g1):
        pl.semaphore_signal(
            barrier, inc=1, device_id=plane_id(plane_peer(offset)), device_id_type=MESH
        )
    for t in range(rounds):
        pl.semaphore_signal(
            barrier, inc=1, device_id=stack_id(stack_peer(t)), device_id_type=MESH
        )
    pl.semaphore_wait(barrier, 2 + g1 - 1 + rounds)

    def halo_pair(source, target, send_sem, recv_sem):
        return [
            remote(
                source.at[..., pl.ds(0, halo), :],
                target.at[..., pl.ds(rows, halo), :],
                send_sem,
                recv_sem,
                {"gy": lower_y},
            ),
            remote(
                source.at[..., pl.ds(rows - halo, halo), :],
                target.at[..., pl.ds(rows + halo, halo), :],
                send_sem,
                recv_sem,
                {"gy": upper_y},
            ),
        ]

    def halos(step, f):
        source = fields.at[f] if step == 0 else present.at[step, f]
        return halo_pair(
            source, present.at[step, f], halo_send.at[step], halo_recv.at[step, f]
        )

    def rate_copy(offset):
        return remote(
            face_rate.at[:, :, lanes(plane_peer(offset))],
            rates_plane.at[mine1],
            rate_send.at[0],
            rate_recv.at[0],
            plane_id(plane_peer(offset)),
        )

    def out1(step, f, offset):
        return remote(
            send1.at[step, plane_peer(offset), f],
            recv1.at[step, mine1, f],
            s1_send.at[step],
            s1_recv.at[step, f],
            plane_id(plane_peer(offset)),
        )

    def in1(step, f, offset):
        return remote(
            back1.at[step, plane_peer(offset), f],
            home1.at[step, mine1, f],
            b1_send.at[step],
            b1_recv.at[step, f],
            plane_id(plane_peer(offset)),
        )

    last = rounds - 1

    def payload2(buffer, step, t, f):
        return buffer.at[step, t, f, pl.ds(0, 1 if t == last else 2)]

    def payload_el(buffer, t, f):
        return buffer.at[t, f, pl.ds(0, 1 if t == last else 3)]

    def pair2(step, t, f):
        return remote(
            payload2(send2, step, t, f),
            payload2(recv2, step, t, f),
            s2_send.at[step, t],
            s2_recv.at[step, t, f],
            stack_id(stack_peer(t)),
        )

    def pair_el(t, f):
        return remote(
            payload_el(send_el, t, f),
            payload_el(recv_el, t, f),
            el_send.at[t],
            el_recv.at[t, f],
            stack_id(stack_peer(t)),
        )

    speed_halos = halo_pair(velocity, speed, speed_send.at[0], speed_recv.at[0])
    for copy in speed_halos:
        copy.start()

    def start_halos(f):
        for copy in halos(0, f):
            copy.start()

    each_field(start_halos)
    for offset in range(1, g1):
        rate_copy(offset).start()

    for copy in locals_in[:3]:
        copy.wait()

    def own_factors(f):
        scale = z_scale[f]
        element = layer_element(scale * rates[0])
        for k in range(1, layers):
            element, factors = join(element, layer_element(scale * rates[k]))
            for n in range(3):
                coef0[n, k - 1, f] = factors[n]

    each_field(own_factors)

    def ring(block):
        place = lax.broadcasted_iota(jnp.int32, (halo, width), 0)
        edge = jnp.where(
            place < halo // 2, block[rows : rows + halo], block[rows + halo : rows + 2 * halo]
        )
        return jnp.concatenate([block[:rows], edge], axis=0)

    for copy in locals_in[3:]:
        copy.wait()
    await_bytes(speed.at[:, :, pl.ds(rows, 2 * halo)], speed_recv.at[0])
    for n in range(2):
        for k in range(layers):
            speed[n, k, : rows + halo] = 0.5 * ring(speed[n, k])

    def plane_factors():
        totals = []
        for f in range(field_total):
            scale = z_scale[f]
            total = None
            for i in range(g1):
                element = layer_element(scale * rates_plane[i, 0])
                for k in range(1, layers):
                    element, ignored = join(element, layer_element(scale * rates_plane[i, k]))
                if total is None:
                    total = element
                else:
                    total, factors = join(total, element)
                    for n in range(3):
                        coef1[n, i - 1, f] = factors[n]
            totals.append(total)
        for f in range(field_total):
            offer_element(0, f, totals[f])
        for f in range(field_total):
            pair_el(0, f).start()

    def offer_element(t, f, element):
        if t < last:
            for n in range(3):
                send_el[t, f, n] = element[n]
        else:
            closing = element[0] + element[2]
            inverse = reciprocal(closing)
            ratio = element[0] * inverse
            coef2[0, t, f] = ratio
            coef2[1, t, f] = inverse
            send_el[t, f, 0] = pick(t, closing, element[1] + ratio * element[2])

    def stack_factors(t):
        for f in range(field_total):
            await_bytes(payload_el(recv_el, t, f), el_recv.at[t, f])
        for f in range(field_total):
            stack_factors_of(t, f)
        if t < last:
            for f in range(field_total):
                pair_el(t + 1, f).start()

    def stack_factors_of(t, f):
        if t < last:
            mine = tuple(send_el[t, f, n] for n in range(3))
            other = tuple(recv_el[t, f, n] for n in range(3))
            lower = tuple(pick(t, a, b) for a, b in zip(mine, other))
            upper = tuple(pick(t, b, a) for a, b in zip(mine, other))
            total, factors = join(lower, upper)
            for n in range(3):
                coef2[n, t, f] = factors[n]
            offer_element(t + 1, f, total)
        else:
            coef2[2, t, f] = reciprocal(send_el[t, f, 0] + recv_el[t, f, 0])

    def own_forward(step, f):
        if step == 0:
            field_in(f).wait()
        await_bytes(present.at[step, f, :, pl.ds(rows, 2 * halo)], halo_recv.at[step, f])
        spread = xy_rate[f]
        centre = 1.0 - 4.0 * spread
        low = None
        high = None
        extent = rows + halo
        for k in range(layers):
            q = ring(present[step, f, k])
            along_x = speed[0, k, :extent]
            along_y = speed[1, k, :extent]
            weights = (
                spread - along_x,
                spread + along_x,
                spread - along_y,
                spread + along_y,
                centre,
            )
            sectioned = stencil(q, pltpu.roll(q, extent - 1, 0), pltpu.roll(q, 1, 0), weights)
            north = pltpu.roll(sectioned, extent - 1, 0)[:rows]
            south = pltpu.roll(sectioned, 1, 0)[:rows]
            inner_weights = tuple(w[:rows] for w in weights[:4]) + (centre,)
            explicit = 0.5 * (
                q[:rows] + stencil(sectioned[:rows], north, south, inner_weights)
            )
            if k == 0:
                high = explicit
            else:
                held0[k - 1, f] = high
                share = coef0[0, k - 1, f] * high
                low = share if low is None else low + share
                high = explicit + coef0[1, k - 1, f] * high
        for c in range(g1):
            cut = slice(c * TILE_LANES, (c + 1) * TILE_LANES)
            send1[step, c, f, 0] = low[:, cut]
            send1[step, c, f, 1] = high[:, cut]
        for offset in range(1, g1):
            out1(step, f, offset).start()
        recv1[step, mine1, f] = send1[step, mine1, f]

    def plane_forward(step, f):
        await_bytes(recv1.at[step, pl.ds(0, g1 - 1), f], s1_recv.at[step, f])
        low = recv1[step, 0, f, 0]
        high = recv1[step, 0, f, 1]
        for i in range(1, g1):
            meeting = high + recv1[step, i, f, 0]
            held1[i - 1, f] = meeting
            low = low + coef1[0, i - 1, f] * meeting
            high = recv1[step, i, f, 1] + coef1[1, i - 1, f] * meeting
        offer(step, 0, f, low, high)

    def offer(step, t, f, low, high):
        if t < last:
            send2[step, t, f, 0] = low
        else:
            send2[step, t, f, 0] = pick(t, high, low + coef2[0, t, f] * high)
        send2[step, t, f, 1] = high
        pair2(step, t, f).start()

    def stack_round(step, t, f):
        await_bytes(payload2(recv2, step, t, f), s2_recv.at[step, t, f])
        low = send2[step, t, f, 0]
        high = send2[step, t, f, 1]
        other_low = recv2[step, t, f, 0]
        if t < last:
            other_high = recv2[step, t, f, 1]
            meeting = pick(t, high, other_high) + pick(t, other_low, low)
            held2[t, f] = meeting
            low, high = (
                pick(t, low, other_low) + coef2[0, t, f] * meeting,
                pick(t, other_high, high) + coef2[1, t, f] * meeting,
            )
            offer(step, t + 1, f, low, high)
            return
        middle = (low + other_low) * coef2[2, t, f]
        top = high * coef2[1, t, f] + coef2[0, t, f] * middle
        base = pick(t, jnp.zeros_like(middle), middle)
        value = pick(t, middle, top)
        for r in range(last - 1, -1, -1):
            middle = (
                held2[r, f] * coef2[2, r, f] + coef2[0, r, f] * base + coef2[1, r, f] * value
            )
            base, value = pick(r, base, middle), pick(r, middle, value)
        back1[step, g1 - 1, f, 1] = value
        for i in range(g1 - 1, 0, -1):
            value = (
                held1[i - 1, f] * coef1[2, i - 1, f]
                + coef1[0, i - 1, f] * base
                + coef1[1, i - 1, f] * value
            )
            back1[step, i, f, 0] = value
            back1[step, i - 1, f, 1] = value
        back1[step, 0, f, 0] = base
        for offset in range(1, g1):
            in1(step, f, offset).start()
        home1[step, mine1, f] = back1[step, mine1, f]

    def own_backward(step, f):
        await_bytes(home1.at[step, pl.ds(0, g1 - 1), f], b1_recv.at[step, f])
        for c in range(g1):
            cut = slice(c * TILE_LANES, (c + 1) * TILE_LANES)
            base = home1[step, c, f, 0]
            value = home1[step, c, f, 1]
            for k in range(layers - 1, -1, -1):
                if k < layers - 1:
                    value = (
                        held0[k, f, :, cut] * coef0[2, k, f, :, cut]
                        + coef0[0, k, f, :, cut] * base
                        + coef0[1, k, f, :, cut] * value
                    )
                if step == STEPS - 1:
                    result[f, k, :, cut] = value
                else:
                    present[step + 1, f, k, :rows, cut] = value
        if step < STEPS - 1:
            for copy in halos(step + 1, f):
                copy.start()
        else:
            field_out(f).start()

    def sent_out(step):
        await_bytes(present.at[step, :, :, pl.ds(rows, 2 * halo)], halo_send.at[step])
        await_bytes(send1.at[step, pl.ds(0, g1 - 1)], s1_send.at[step])
        for t in range(rounds):
            await_bytes(send2.at[step, t, :, pl.ds(0, 1 if t == last else 2)], s2_send.at[step, t])

    def sent_home(step):
        await_bytes(back1.at[step, pl.ds(0, g1 - 1)], b1_send.at[step])

    each_field(functools.partial(own_forward, 0))
    await_bytes(rates_plane.at[pl.ds(0, g1 - 1)], rate_recv.at[0])
    plane_factors()
    for step in range(STEPS):
        each_field(functools.partial(plane_forward, step))
        for t in range(rounds):
            if step == 0:
                stack_factors(t)
            each_field(functools.partial(stack_round, step, t))
        if step == 0:
            await_bytes(speed.at[:, :, pl.ds(rows, 2 * halo)], speed_send.at[0])
            await_bytes(rates_plane.at[pl.ds(0, g1 - 1)], rate_send.at[0])
            for t in range(rounds):
                await_bytes(send_el.at[t, :, pl.ds(0, 1 if t == last else 3)], el_send.at[t])
        sent_out(step)
        if step < STEPS - 1:
            own_backward(step, 0)

            def turn(f, carry, step=step):
                own_backward(step, f)
                own_forward(step + 1, f - 1)
                return carry

            lax.fori_loop(1, field_total, turn, 0)
            own_forward(step + 1, field_total - 1)
            sent_home(step)
        else:
            each_field(functools.partial(own_backward, step))
            sent_home(step)
            each_field(lambda f: field_out(f).wait())


def on_device(fields, velocity, face_rate, xy_rate, z_scale):
    gz_count = lax.axis_size("gz")
    gy_count = lax.axis_size("gy")
    field_total, layers, rows, width = fields.shape
    g1 = width // TILE_LANES
    g2 = gz_count // g1
    rounds = g2.bit_length() - 1
    assert g1 * 2**rounds == gz_count
    plan = (g1, g2, rounds, gy_count)
    extent = rows + 2 * TILE_ROWS
    share1 = (rows, TILE_LANES)
    vmem = lambda *shape: pltpu.VMEM(shape, jnp.float32)
    dma = lambda *shape: pltpu.SemaphoreType.DMA(shape)
    return pl.pallas_call(
        functools.partial(kernel, plan),
        out_shape=jax.ShapeDtypeStruct(fields.shape, jnp.float32),
        in_specs=[pl.BlockSpec(memory_space=pl.ANY)] * 5,
        out_specs=pl.BlockSpec(memory_space=pl.ANY),
        scratch_shapes=[
            pltpu.SMEM((field_total,), jnp.float32),
            pltpu.SMEM((field_total,), jnp.float32),
            vmem(STEPS, field_total, layers, extent, width),
            vmem(2, layers, extent, width),
            vmem(layers, rows, width),
            vmem(g1, layers, rows, TILE_LANES),
            vmem(3, layers - 1, field_total, rows, width),
            vmem(layers - 1, field_total, rows, width),
            vmem(3, g1 - 1, field_total, *share1),
            vmem(g1 - 1, field_total, *share1),
            vmem(3, rounds, field_total, *share1),
            vmem(rounds, field_total, *share1),
            vmem(field_total, layers, rows, width),
            vmem(STEPS, g1, field_total, 2, *share1),
            vmem(STEPS, g1, field_total, 2, *share1),
            vmem(STEPS, g1, field_total, 2, *share1),
            vmem(STEPS, g1, field_total, 2, *share1),
            vmem(STEPS, rounds, field_total, 2, *share1),
            vmem(STEPS, rounds, field_total, 2, *share1),
            vmem(rounds, field_total, 3, *share1),
            vmem(rounds, field_total, 3, *share1),
            dma(5),
            dma(field_total),
            dma(field_total),
            dma(STEPS),
            dma(STEPS, field_total),
            dma(1),
            dma(1),
            dma(1),
            dma(1),
            dma(STEPS),
            dma(STEPS, field_total),
            dma(STEPS),
            dma(STEPS, field_total),
            dma(STEPS, rounds),
            dma(STEPS, rounds, field_total),
            dma(rounds),
            dma(rounds, field_total),
        ],
        compiler_params=pltpu.CompilerParams(
            collective_id=0, has_side_effects=True, vmem_limit_bytes=60 * 1024 * 1024
        ),
        cost_estimate=pl.CostEstimate(
            flops=400 * fields.size, bytes_accessed=16 * fields.size, transcendentals=0
        ),
    )(xy_rate, z_scale, fields, velocity, face_rate)


def solution(mesh):
    in_specs = (P(None, "gz", "gy", None), P(None, "gz", "gy", None), P("gz", "gy", None), P(), P())
    out_specs = P(None, "gz", "gy", None)
    return jax.shard_map(
        on_device, mesh=mesh, in_specs=in_specs, out_specs=out_specs, check_vma=False
    )
```

```python
import functools

import jax
import jax.numpy as jnp
from jax import lax
from jax.experimental import pallas as pl
from jax.experimental.pallas import tpu as pltpu
from jax.sharding import PartitionSpec as P

STEPS = 2
TILE_ROWS = 8
TILE_LANES = 128
EDGE = 2
MESH = pl.DeviceIdType.MESH


def stencil(q, north, south, weights):
    width = q.shape[1]
    east, west, up, down, centre = weights
    eastern = pltpu.roll(q, width - 1, 1)
    western = pltpu.roll(q, 1, 1)
    return (east * eastern + west * western) + (up * north + down * south) + centre * q


def reciprocal(value):
    estimate = pl.reciprocal(value, approx=True)
    estimate = estimate * (2.0 - value * estimate)
    return estimate * (2.0 - value * estimate)


def join(lower, upper):
    between = lower[2] + upper[1]
    inverse = reciprocal(lower[0] + upper[0] + between)
    to_low = lower[0] * inverse
    to_high = upper[0] * inverse
    element = (to_low * upper[0], lower[1] + to_low * between, upper[2] + to_high * between)
    return element, (to_low, to_high, inverse)


def layer_element(rate):
    return (rate, jnp.zeros_like(rate), jnp.ones_like(rate))


def kernel(
    plan,
    xy_hbm,
    z_hbm,
    fields,
    velocity,
    face_rate,
    out,
    xy_rate,
    z_scale,
    present,
    speed,
    rates,
    rates_plane,
    coef0,
    held0,
    coef1,
    held1,
    coef2,
    held2,
    result,
    send1,
    recv1,
    back1,
    home1,
    send2,
    recv2,
    send_el,
    recv_el,
    local_sem,
    field_sem,
    out_sem,
    halo_send,
    halo_recv,
    speed_send,
    speed_recv,
    rate_send,
    rate_recv,
    s1_send,
    s1_recv,
    b1_send,
    b1_recv,
    s2_send,
    s2_recv,
    el_send,
    el_recv,
):
    g1, g2, rounds, gy_count = plan
    field_total, layers, rows, width = fields.shape
    halo = TILE_ROWS
    me = lax.axis_index("gz")
    my_y = lax.axis_index("gy")
    mine1 = lax.rem(me, g1)
    mine2 = lax.div(me, g1)
    upper_y = lax.rem(my_y + 1, gy_count)
    lower_y = lax.rem(my_y + gy_count - 1, gy_count)

    def plane_peer(offset):
        return lax.rem(mine1 + offset, g1)

    def stack_bit(t):
        return lax.rem(lax.div(mine2, 2**t), 2)

    def stack_peer(t):
        return mine2 + (1 - 2 * stack_bit(t)) * 2**t

    def pick(t, lower, upper):
        return jnp.where(jnp.broadcast_to(stack_bit(t), lower.shape) == 0, lower, upper)

    def plane_id(position):
        return {"gz": mine2 * g1 + position}

    def stack_id(position):
        return {"gz": position * g1 + mine1}

    def lanes(position):
        return pl.ds(pl.multiple_of(position * TILE_LANES, TILE_LANES), TILE_LANES)

    def each_field(body):
        def step_body(f, carry):
            body(f)
            return carry

        lax.fori_loop(0, field_total, step_body, 0)

    def remote(source, target, send_sem, recv_sem, device):
        return pltpu.make_async_remote_copy(
            src_ref=source,
            dst_ref=target,
            send_sem=send_sem,
            recv_sem=recv_sem,
            device_id=device,
            device_id_type=MESH,
        )

    def await_bytes(ref, semaphore):
        pltpu.make_async_copy(ref, ref, semaphore).wait()

    def field_in(f):
        return pltpu.make_async_copy(
            fields.at[f], present.at[0, f, :, pl.ds(0, rows)], field_sem.at[f]
        )

    def field_out(f):
        return pltpu.make_async_copy(result.at[f], out.at[f], out_sem.at[f])

    for ref in (present, speed):
        ref[..., rows:, :] = jnp.zeros(ref.shape[:-2] + (halo, width), jnp.float32)

    locals_in = [
        pltpu.make_async_copy(z_hbm, z_scale, local_sem.at[0]),
        pltpu.make_async_copy(xy_hbm, xy_rate, local_sem.at[1]),
        pltpu.make_async_copy(face_rate, rates, local_sem.at[2]),
        pltpu.make_async_copy(velocity, speed.at[:, :, pl.ds(0, rows)], local_sem.at[3]),
        pltpu.make_async_copy(
            face_rate.at[:, :, lanes(mine1)], rates_plane.at[mine1], local_sem.at[4]
        ),
    ]
    for copy in locals_in:
        copy.start()
    each_field(lambda f: field_in(f).start())

    barrier = pltpu.get_barrier_semaphore()
    for target in (lower_y, upper_y):
        pl.semaphore_signal(barrier, inc=1, device_id={"gy": target}, device_id_type=MESH)
    for offset in range(1, g1):
        pl.semaphore_signal(
            barrier, inc=1, device_id=plane_id(plane_peer(offset)), device_id_type=MESH
        )
    for t in range(rounds):
        pl.semaphore_signal(
            barrier, inc=1, device_id=stack_id(stack_peer(t)), device_id_type=MESH
        )
    pl.semaphore_wait(barrier, 2 + g1 - 1 + rounds)

    def halo_pair(source, target, send_sem, recv_sem):
        return [
            remote(
                source.at[..., pl.ds(0, EDGE), :],
                target.at[..., pl.ds(rows, EDGE), :],
                send_sem,
                recv_sem,
                {"gy": lower_y},
            ),
            remote(
                source.at[..., pl.ds(rows - EDGE, EDGE), :],
                target.at[..., pl.ds(rows + halo - EDGE, EDGE), :],
                send_sem,
                recv_sem,
                {"gy": upper_y},
            ),
        ]

    def halos(step, f):
        source = fields.at[f] if step == 0 else present.at[step, f]
        return halo_pair(
            source, present.at[step, f], halo_send.at[step], halo_recv.at[step, f]
        )

    def rate_copy(offset):
        return remote(
            face_rate.at[:, :, lanes(plane_peer(offset))],
            rates_plane.at[mine1],
            rate_send.at[0],
            rate_recv.at[0],
            plane_id(plane_peer(offset)),
        )

    def out1(step, f, offset):
        return remote(
            send1.at[step, plane_peer(offset), f],
            recv1.at[step, mine1, f],
            s1_send.at[step],
            s1_recv.at[step, f],
            plane_id(plane_peer(offset)),
        )

    def in1(step, f, offset):
        return remote(
            back1.at[step, plane_peer(offset), f],
            home1.at[step, mine1, f],
            b1_send.at[step],
            b1_recv.at[step, f],
            plane_id(plane_peer(offset)),
        )

    last = rounds - 1

    def payload2(buffer, step, t, f):
        return buffer.at[step, t, f, pl.ds(0, 1 if t == last else 2)]

    def payload_el(buffer, t, f):
        return buffer.at[t, f, pl.ds(0, 1 if t == last else 3)]

    def pair2(step, t, f):
        return remote(
            payload2(send2, step, t, f),
            payload2(recv2, step, t, f),
            s2_send.at[step, t],
            s2_recv.at[step, t, f],
            stack_id(stack_peer(t)),
        )

    def pair_el(t, f):
        return remote(
            payload_el(send_el, t, f),
            payload_el(recv_el, t, f),
            el_send.at[t],
            el_recv.at[t, f],
            stack_id(stack_peer(t)),
        )

    speed_halos = halo_pair(velocity, speed, speed_send.at[0], speed_recv.at[0])
    for copy in speed_halos:
        copy.start()

    def start_halos(f):
        for copy in halos(0, f):
            copy.start()

    each_field(start_halos)
    for offset in range(1, g1):
        rate_copy(offset).start()

    for copy in locals_in[:3]:
        copy.wait()

    def own_factors(f):
        scale = z_scale[f]
        element = layer_element(scale * rates[0])
        for k in range(1, layers):
            element, factors = join(element, layer_element(scale * rates[k]))
            for n in range(3):
                coef0[n, k - 1, f] = factors[n]

    each_field(own_factors)

    for copy in locals_in[3:]:
        copy.wait()
    await_bytes(speed.at[:, :, pl.ds(0, 2 * EDGE)], speed_recv.at[0])
    for n in range(2):
        for k in range(layers):
            speed[n, k] = 0.5 * speed[n, k]

    def plane_factors():
        totals = []
        for f in range(field_total):
            scale = z_scale[f]
            total = None
            for i in range(g1):
                element = layer_element(scale * rates_plane[i, 0])
                for k in range(1, layers):
                    element, ignored = join(element, layer_element(scale * rates_plane[i, k]))
                if total is None:
                    total = element
                else:
                    total, factors = join(total, element)
                    for n in range(3):
                        coef1[n, i - 1, f] = factors[n]
            totals.append(total)
        for f in range(field_total):
            offer_element(0, f, totals[f])
        for f in range(field_total):
            pair_el(0, f).start()

    def offer_element(t, f, element):
        if t < last:
            for n in range(3):
                send_el[t, f, n] = element[n]
        else:
            closing = element[0] + element[2]
            inverse = reciprocal(closing)
            ratio = element[0] * inverse
            coef2[0, t, f] = ratio
            coef2[1, t, f] = inverse
            send_el[t, f, 0] = pick(t, closing, element[1] + ratio * element[2])

    def stack_factors(t):
        for f in range(field_total):
            await_bytes(payload_el(recv_el, t, f), el_recv.at[t, f])
        for f in range(field_total):
            stack_factors_of(t, f)
        if t < last:
            for f in range(field_total):
                pair_el(t + 1, f).start()

    def stack_factors_of(t, f):
        if t < last:
            mine = tuple(send_el[t, f, n] for n in range(3))
            other = tuple(recv_el[t, f, n] for n in range(3))
            lower = tuple(pick(t, a, b) for a, b in zip(mine, other))
            upper = tuple(pick(t, b, a) for a, b in zip(mine, other))
            total, factors = join(lower, upper)
            for n in range(3):
                coef2[n, t, f] = factors[n]
            offer_element(t + 1, f, total)
        else:
            coef2[2, t, f] = reciprocal(send_el[t, f, 0] + recv_el[t, f, 0])

    def own_forward(step, f):
        if step == 0:
            field_in(f).wait()
        await_bytes(present.at[step, f, :, pl.ds(0, 2 * EDGE)], halo_recv.at[step, f])
        spread = xy_rate[f]
        centre = 1.0 - 4.0 * spread
        low = None
        high = None
        extent = rows + halo
        for k in range(layers):
            q = present[step, f, k]
            along_x = speed[0, k]
            along_y = speed[1, k]
            weights = (
                spread - along_x,
                spread + along_x,
                spread - along_y,
                spread + along_y,
                centre,
            )
            sectioned = stencil(q, pltpu.roll(q, extent - 1, 0), pltpu.roll(q, 1, 0), weights)
            north = pltpu.roll(sectioned, extent - 1, 0)[:rows]
            south = pltpu.roll(sectioned, 1, 0)[:rows]
            inner_weights = tuple(w[:rows] for w in weights[:4]) + (centre,)
            explicit = 0.5 * (
                q[:rows] + stencil(sectioned[:rows], north, south, inner_weights)
            )
            if k == 0:
                high = explicit
            else:
                held0[k - 1, f] = high
                share = coef0[0, k - 1, f] * high
                low = share if low is None else low + share
                high = explicit + coef0[1, k - 1, f] * high
        for c in range(g1):
            cut = slice(c * TILE_LANES, (c + 1) * TILE_LANES)
            send1[step, c, f, 0] = low[:, cut]
            send1[step, c, f, 1] = high[:, cut]
        for offset in range(1, g1):
            out1(step, f, offset).start()
        recv1[step, mine1, f] = send1[step, mine1, f]

    def plane_forward(step, f):
        await_bytes(recv1.at[step, pl.ds(0, g1 - 1), f], s1_recv.at[step, f])
        low = recv1[step, 0, f, 0]
        high = recv1[step, 0, f, 1]
        for i in range(1, g1):
            meeting = high + recv1[step, i, f, 0]
            held1[i - 1, f] = meeting
            low = low + coef1[0, i - 1, f] * meeting
            high = recv1[step, i, f, 1] + coef1[1, i - 1, f] * meeting
        offer(step, 0, f, low, high)

    def offer(step, t, f, low, high):
        if t < last:
            send2[step, t, f, 0] = low
        else:
            send2[step, t, f, 0] = pick(t, high, low + coef2[0, t, f] * high)
        send2[step, t, f, 1] = high
        pair2(step, t, f).start()

    def stack_round(step, t, f):
        await_bytes(payload2(recv2, step, t, f), s2_recv.at[step, t, f])
        low = send2[step, t, f, 0]
        high = send2[step, t, f, 1]
        other_low = recv2[step, t, f, 0]
        if t < last:
            other_high = recv2[step, t, f, 1]
            meeting = pick(t, high, other_high) + pick(t, other_low, low)
            held2[t, f] = meeting
            low, high = (
                pick(t, low, other_low) + coef2[0, t, f] * meeting,
                pick(t, other_high, high) + coef2[1, t, f] * meeting,
            )
            offer(step, t + 1, f, low, high)
            return
        middle = (low + other_low) * coef2[2, t, f]
        top = high * coef2[1, t, f] + coef2[0, t, f] * middle
        base = pick(t, jnp.zeros_like(middle), middle)
        value = pick(t, middle, top)
        for r in range(last - 1, -1, -1):
            middle = (
                held2[r, f] * coef2[2, r, f] + coef2[0, r, f] * base + coef2[1, r, f] * value
            )
            base, value = pick(r, base, middle), pick(r, middle, value)
        back1[step, g1 - 1, f, 1] = value
        for i in range(g1 - 1, 0, -1):
            value = (
                held1[i - 1, f] * coef1[2, i - 1, f]
                + coef1[0, i - 1, f] * base
                + coef1[1, i - 1, f] * value
            )
            back1[step, i, f, 0] = value
            back1[step, i - 1, f, 1] = value
        back1[step, 0, f, 0] = base
        for offset in range(1, g1):
            in1(step, f, offset).start()
        home1[step, mine1, f] = back1[step, mine1, f]

    def own_backward(step, f):
        await_bytes(home1.at[step, pl.ds(0, g1 - 1), f], b1_recv.at[step, f])
        for c in range(g1):
            cut = slice(c * TILE_LANES, (c + 1) * TILE_LANES)
            base = home1[step, c, f, 0]
            value = home1[step, c, f, 1]
            for k in range(layers - 1, -1, -1):
                if k < layers - 1:
                    value = (
                        held0[k, f, :, cut] * coef0[2, k, f, :, cut]
                        + coef0[0, k, f, :, cut] * base
                        + coef0[1, k, f, :, cut] * value
                    )
                if step == STEPS - 1:
                    result[f, k, :, cut] = value
                else:
                    present[step + 1, f, k, :rows, cut] = value
        if step < STEPS - 1:
            for copy in halos(step + 1, f):
                copy.start()
        else:
            field_out(f).start()

    def sent_out(step):
        await_bytes(present.at[step, :, :, pl.ds(0, 2 * EDGE)], halo_send.at[step])
        await_bytes(send1.at[step, pl.ds(0, g1 - 1)], s1_send.at[step])
        for t in range(rounds):
            await_bytes(send2.at[step, t, :, pl.ds(0, 1 if t == last else 2)], s2_send.at[step, t])

    def sent_home(step):
        await_bytes(back1.at[step, pl.ds(0, g1 - 1)], b1_send.at[step])

    each_field(functools.partial(own_forward, 0))
    await_bytes(rates_plane.at[pl.ds(0, g1 - 1)], rate_recv.at[0])
    plane_factors()
    for step in range(STEPS):
        each_field(functools.partial(plane_forward, step))
        for t in range(rounds):
            if step == 0:
                stack_factors(t)
            each_field(functools.partial(stack_round, step, t))
        if step == 0:
            await_bytes(speed.at[:, :, pl.ds(0, 2 * EDGE)], speed_send.at[0])
            await_bytes(rates_plane.at[pl.ds(0, g1 - 1)], rate_send.at[0])
            for t in range(rounds):
                await_bytes(send_el.at[t, :, pl.ds(0, 1 if t == last else 3)], el_send.at[t])
        sent_out(step)
        if step < STEPS - 1:
            own_backward(step, 0)

            def turn(f, carry, step=step):
                own_backward(step, f)
                own_forward(step + 1, f - 1)
                return carry

            lax.fori_loop(1, field_total, turn, 0)
            own_forward(step + 1, field_total - 1)
            sent_home(step)
        else:
            each_field(functools.partial(own_backward, step))
            sent_home(step)
            each_field(lambda f: field_out(f).wait())


def on_device(fields, velocity, face_rate, xy_rate, z_scale):
    gz_count = lax.axis_size("gz")
    gy_count = lax.axis_size("gy")
    field_total, layers, rows, width = fields.shape
    g1 = width // TILE_LANES
    g2 = gz_count // g1
    rounds = g2.bit_length() - 1
    assert g1 * 2**rounds == gz_count
    plan = (g1, g2, rounds, gy_count)
    extent = rows + TILE_ROWS
    share1 = (rows, TILE_LANES)
    vmem = lambda *shape: pltpu.VMEM(shape, jnp.float32)
    dma = lambda *shape: pltpu.SemaphoreType.DMA(shape)
    return pl.pallas_call(
        functools.partial(kernel, plan),
        out_shape=jax.ShapeDtypeStruct(fields.shape, jnp.float32),
        in_specs=[pl.BlockSpec(memory_space=pl.ANY)] * 5,
        out_specs=pl.BlockSpec(memory_space=pl.ANY),
        scratch_shapes=[
            pltpu.SMEM((field_total,), jnp.float32),
            pltpu.SMEM((field_total,), jnp.float32),
            vmem(STEPS, field_total, layers, extent, width),
            vmem(2, layers, extent, width),
            vmem(layers, rows, width),
            vmem(g1, layers, rows, TILE_LANES),
            vmem(3, layers - 1, field_total, rows, width),
            vmem(layers - 1, field_total, rows, width),
            vmem(3, g1 - 1, field_total, *share1),
            vmem(g1 - 1, field_total, *share1),
            vmem(3, rounds, field_total, *share1),
            vmem(rounds, field_total, *share1),
            vmem(field_total, layers, rows, width),
            vmem(STEPS, g1, field_total, 2, *share1),
            vmem(STEPS, g1, field_total, 2, *share1),
            vmem(STEPS, g1, field_total, 2, *share1),
            vmem(STEPS, g1, field_total, 2, *share1),
            vmem(STEPS, rounds, field_total, 2, *share1),
            vmem(STEPS, rounds, field_total, 2, *share1),
            vmem(rounds, field_total, 3, *share1),
            vmem(rounds, field_total, 3, *share1),
            dma(5),
            dma(field_total),
            dma(field_total),
            dma(STEPS),
            dma(STEPS, field_total),
            dma(1),
            dma(1),
            dma(1),
            dma(1),
            dma(STEPS),
            dma(STEPS, field_total),
            dma(STEPS),
            dma(STEPS, field_total),
            dma(STEPS, rounds),
            dma(STEPS, rounds, field_total),
            dma(rounds),
            dma(rounds, field_total),
        ],
        compiler_params=pltpu.CompilerParams(
            collective_id=0, has_side_effects=True, vmem_limit_bytes=60 * 1024 * 1024
        ),
        cost_estimate=pl.CostEstimate(
            flops=400 * fields.size, bytes_accessed=16 * fields.size, transcendentals=0
        ),
    )(xy_rate, z_scale, fields, velocity, face_rate)


def solution(mesh):
    in_specs = (P(None, "gz", "gy", None), P(None, "gz", "gy", None), P("gz", "gy", None), P(), P())
    out_specs = P(None, "gz", "gy", None)
    return jax.shard_map(
        on_device, mesh=mesh, in_specs=in_specs, out_specs=out_specs, check_vma=False
    )
```

```python
import functools

import jax
import jax.numpy as jnp
from jax import lax
from jax.experimental import pallas as pl
from jax.experimental.pallas import tpu as pltpu
from jax.sharding import PartitionSpec as P

STEPS = 2
TILE_ROWS = 8
TILE_LANES = 128
EDGE = 2
MESH = pl.DeviceIdType.MESH


def stencil(q, north, south, weights):
    width = q.shape[1]
    east, west, up, down, centre = weights
    eastern = pltpu.roll(q, width - 1, 1)
    western = pltpu.roll(q, 1, 1)
    return (east * eastern + west * western) + (up * north + down * south) + centre * q


def reciprocal(value):
    estimate = pl.reciprocal(value, approx=True)
    estimate = estimate * (2.0 - value * estimate)
    return estimate * (2.0 - value * estimate)


def join(lower, upper):
    between = lower[2] + upper[1]
    inverse = reciprocal(lower[0] + upper[0] + between)
    to_low = lower[0] * inverse
    to_high = upper[0] * inverse
    element = (to_low * upper[0], lower[1] + to_low * between, upper[2] + to_high * between)
    return element, (to_low, to_high, inverse)


def layer_element(rate):
    return (rate, jnp.zeros_like(rate), jnp.ones_like(rate))


def kernel(
    plan,
    xy_hbm,
    z_hbm,
    fields,
    velocity,
    face_rate,
    out,
    xy_rate,
    z_scale,
    present,
    speed,
    rates,
    rates_plane,
    coef0,
    held0,
    coef1,
    held1,
    coef2,
    held2,
    result,
    send1,
    recv1,
    back1,
    home1,
    send2,
    recv2,
    send_el,
    recv_el,
    local_sem,
    field_sem,
    out_sem,
    halo_send,
    halo_recv,
    speed_send,
    speed_recv,
    rate_send,
    rate_recv,
    s1_send,
    s1_recv,
    b1_send,
    b1_recv,
    s2_send,
    s2_recv,
    el_send,
    el_recv,
):
    g1, g2, rounds, gy_count, chunk = plan
    field_total, layers, rows, width = fields.shape
    halo = TILE_ROWS
    me = lax.axis_index("gz")
    my_y = lax.axis_index("gy")
    mine1 = lax.rem(me, g1)
    mine2 = lax.div(me, g1)
    upper_y = lax.rem(my_y + 1, gy_count)
    lower_y = lax.rem(my_y + gy_count - 1, gy_count)

    def plane_peer(offset):
        return lax.rem(mine1 + offset, g1)

    def stack_bit(t):
        return lax.rem(lax.div(mine2, 2**t), 2)

    def stack_peer(t):
        return mine2 + (1 - 2 * stack_bit(t)) * 2**t

    def pick(t, lower, upper):
        return jnp.where(jnp.broadcast_to(stack_bit(t), lower.shape) == 0, lower, upper)

    def plane_id(position):
        return {"gz": mine2 * g1 + position}

    def stack_id(position):
        return {"gz": position * g1 + mine1}

    def lanes(position):
        return pl.ds(pl.multiple_of(position * TILE_LANES, TILE_LANES), TILE_LANES)

    def each_field(body):
        def step_body(f, carry):
            body(f)
            return carry

        lax.fori_loop(0, field_total, step_body, 0)

    def each_chunk(body):
        def step_body(c, carry):
            body(c)
            return carry

        lax.fori_loop(0, field_total // chunk, step_body, 0)

    def of_chunk(c):
        return pl.ds(c * chunk, chunk)

    def remote(source, target, send_sem, recv_sem, device):
        return pltpu.make_async_remote_copy(
            src_ref=source,
            dst_ref=target,
            send_sem=send_sem,
            recv_sem=recv_sem,
            device_id=device,
            device_id_type=MESH,
        )

    def await_bytes(ref, semaphore):
        pltpu.make_async_copy(ref, ref, semaphore).wait()

    def field_in(f):
        return pltpu.make_async_copy(
            fields.at[f], present.at[0, f, :, pl.ds(0, rows)], field_sem.at[f]
        )

    def field_out(f):
        return pltpu.make_async_copy(result.at[f], out.at[f], out_sem.at[f])

    for ref in (present, speed):
        ref[..., rows:, :] = jnp.zeros(ref.shape[:-2] + (halo, width), jnp.float32)

    locals_in = [
        pltpu.make_async_copy(z_hbm, z_scale, local_sem.at[0]),
        pltpu.make_async_copy(xy_hbm, xy_rate, local_sem.at[1]),
        pltpu.make_async_copy(face_rate, rates, local_sem.at[2]),
        pltpu.make_async_copy(velocity, speed.at[:, :, pl.ds(0, rows)], local_sem.at[3]),
        pltpu.make_async_copy(
            face_rate.at[:, :, lanes(mine1)], rates_plane.at[mine1], local_sem.at[4]
        ),
    ]
    for copy in locals_in:
        copy.start()
    each_field(lambda f: field_in(f).start())

    barrier = pltpu.get_barrier_semaphore()
    for target in (lower_y, upper_y):
        pl.semaphore_signal(barrier, inc=1, device_id={"gy": target}, device_id_type=MESH)
    for offset in range(1, g1):
        pl.semaphore_signal(
            barrier, inc=1, device_id=plane_id(plane_peer(offset)), device_id_type=MESH
        )
    for t in range(rounds):
        pl.semaphore_signal(
            barrier, inc=1, device_id=stack_id(stack_peer(t)), device_id_type=MESH
        )
    pl.semaphore_wait(barrier, 2 + g1 - 1 + rounds)

    def halo_pair(source, target, send_sem, recv_sem):
        return [
            remote(
                source.at[..., pl.ds(0, EDGE), :],
                target.at[..., pl.ds(rows, EDGE), :],
                send_sem,
                recv_sem,
                {"gy": lower_y},
            ),
            remote(
                source.at[..., pl.ds(rows - EDGE, EDGE), :],
                target.at[..., pl.ds(rows + halo - EDGE, EDGE), :],
                send_sem,
                recv_sem,
                {"gy": upper_y},
            ),
        ]

    def halos(step, f):
        source = fields.at[f] if step == 0 else present.at[step, f]
        return halo_pair(
            source, present.at[step, f], halo_send.at[step], halo_recv.at[step, f]
        )

    def rate_copy(offset):
        return remote(
            face_rate.at[:, :, lanes(plane_peer(offset))],
            rates_plane.at[mine1],
            rate_send.at[0],
            rate_recv.at[0],
            plane_id(plane_peer(offset)),
        )

    def out1(step, c, offset):
        return remote(
            send1.at[step, plane_peer(offset), of_chunk(c)],
            recv1.at[step, mine1, of_chunk(c)],
            s1_send.at[step],
            s1_recv.at[step, c],
            plane_id(plane_peer(offset)),
        )

    def in1(step, c, offset):
        return remote(
            back1.at[step, plane_peer(offset), of_chunk(c)],
            home1.at[step, mine1, of_chunk(c)],
            b1_send.at[step],
            b1_recv.at[step, c],
            plane_id(plane_peer(offset)),
        )

    last = rounds - 1

    def payload2(buffer, step, t, c):
        return buffer.at[step, t, c, pl.ds(0, 1 if t == last else 2)]

    def payload_el(buffer, t, f):
        return buffer.at[t, f, pl.ds(0, 1 if t == last else 3)]

    def pair2(step, t, c):
        return remote(
            payload2(send2, step, t, c),
            payload2(recv2, step, t, c),
            s2_send.at[step, t],
            s2_recv.at[step, t, c],
            stack_id(stack_peer(t)),
        )

    def pair_el(t, f):
        return remote(
            payload_el(send_el, t, f),
            payload_el(recv_el, t, f),
            el_send.at[t],
            el_recv.at[t, f],
            stack_id(stack_peer(t)),
        )

    speed_halos = halo_pair(velocity, speed, speed_send.at[0], speed_recv.at[0])
    for copy in speed_halos:
        copy.start()

    def start_halos(f):
        for copy in halos(0, f):
            copy.start()

    each_field(start_halos)
    for offset in range(1, g1):
        rate_copy(offset).start()

    for copy in locals_in[:3]:
        copy.wait()

    def own_factors(f):
        scale = z_scale[f]
        element = layer_element(scale * rates[0])
        for k in range(1, layers):
            element, factors = join(element, layer_element(scale * rates[k]))
            for n in range(3):
                coef0[n, k - 1, f] = factors[n]

    each_field(own_factors)

    for copy in locals_in[3:]:
        copy.wait()
    await_bytes(speed.at[:, :, pl.ds(0, 2 * EDGE)], speed_recv.at[0])
    for n in range(2):
        for k in range(layers):
            speed[n, k] = 0.5 * speed[n, k]

    def plane_factors():
        totals = []
        for f in range(field_total):
            scale = z_scale[f]
            total = None
            for i in range(g1):
                element = layer_element(scale * rates_plane[i, 0])
                for k in range(1, layers):
                    element, ignored = join(element, layer_element(scale * rates_plane[i, k]))
                if total is None:
                    total = element
                else:
                    total, factors = join(total, element)
                    for n in range(3):
                        coef1[n, i - 1, f] = factors[n]
            totals.append(total)
        for f in range(field_total):
            offer_element(0, f, totals[f])
        for f in range(field_total):
            pair_el(0, f).start()

    def offer_element(t, f, element):
        if t < last:
            for n in range(3):
                send_el[t, f, n] = element[n]
        else:
            closing = element[0] + element[2]
            inverse = reciprocal(closing)
            ratio = element[0] * inverse
            coef2[0, t, f] = ratio
            coef2[1, t, f] = inverse
            send_el[t, f, 0] = pick(t, closing, element[1] + ratio * element[2])

    def stack_factors(t):
        for f in range(field_total):
            await_bytes(payload_el(recv_el, t, f), el_recv.at[t, f])
        for f in range(field_total):
            stack_factors_of(t, f)
        if t < last:
            for f in range(field_total):
                pair_el(t + 1, f).start()

    def stack_factors_of(t, f):
        if t < last:
            mine = tuple(send_el[t, f, n] for n in range(3))
            other = tuple(recv_el[t, f, n] for n in range(3))
            lower = tuple(pick(t, a, b) for a, b in zip(mine, other))
            upper = tuple(pick(t, b, a) for a, b in zip(mine, other))
            total, factors = join(lower, upper)
            for n in range(3):
                coef2[n, t, f] = factors[n]
            offer_element(t + 1, f, total)
        else:
            coef2[2, t, f] = reciprocal(send_el[t, f, 0] + recv_el[t, f, 0])

    def own_forward(step, f):
        if step == 0:
            field_in(f).wait()
        await_bytes(present.at[step, f, :, pl.ds(0, 2 * EDGE)], halo_recv.at[step, f])
        spread = xy_rate[f]
        centre = 1.0 - 4.0 * spread
        low = None
        high = None
        extent = rows + halo
        for k in range(layers):
            q = present[step, f, k]
            along_x = speed[0, k]
            along_y = speed[1, k]
            weights = (
                spread - along_x,
                spread + along_x,
                spread - along_y,
                spread + along_y,
                centre,
            )
            sectioned = stencil(q, pltpu.roll(q, extent - 1, 0), pltpu.roll(q, 1, 0), weights)
            north = pltpu.roll(sectioned, extent - 1, 0)[:rows]
            south = pltpu.roll(sectioned, 1, 0)[:rows]
            inner_weights = tuple(w[:rows] for w in weights[:4]) + (centre,)
            explicit = 0.5 * (
                q[:rows] + stencil(sectioned[:rows], north, south, inner_weights)
            )
            if k == 0:
                high = explicit
            else:
                held0[k - 1, f] = high
                share = coef0[0, k - 1, f] * high
                low = share if low is None else low + share
                high = explicit + coef0[1, k - 1, f] * high
        for c in range(g1):
            cut = slice(c * TILE_LANES, (c + 1) * TILE_LANES)
            send1[step, c, f, 0] = low[:, cut]
            send1[step, c, f, 1] = high[:, cut]
        recv1[step, mine1, f] = send1[step, mine1, f]

        @pl.when(lax.rem(f, chunk) == chunk - 1)
        def send():
            for offset in range(1, g1):
                out1(step, lax.div(f, chunk), offset).start()

    def plane_forward(step, c):
        fs = of_chunk(c)
        await_bytes(recv1.at[step, pl.ds(0, g1 - 1), fs], s1_recv.at[step, c])
        low = recv1[step, 0, fs, 0]
        high = recv1[step, 0, fs, 1]
        for i in range(1, g1):
            meeting = high + recv1[step, i, fs, 0]
            held1[i - 1, fs] = meeting
            low = low + coef1[0, i - 1, fs] * meeting
            high = recv1[step, i, fs, 1] + coef1[1, i - 1, fs] * meeting
        offer(step, 0, c, low, high)

    def offer(step, t, c, low, high):
        fs = of_chunk(c)
        if t < last:
            send2[step, t, c, 0] = low
        else:
            send2[step, t, c, 0] = pick(t, high, low + coef2[0, t, fs] * high)
        send2[step, t, c, 1] = high
        pair2(step, t, c).start()

    def stack_round(step, t, c):
        fs = of_chunk(c)
        await_bytes(payload2(recv2, step, t, c), s2_recv.at[step, t, c])
        low = send2[step, t, c, 0]
        high = send2[step, t, c, 1]
        other_low = recv2[step, t, c, 0]
        if t < last:
            other_high = recv2[step, t, c, 1]
            meeting = pick(t, high, other_high) + pick(t, other_low, low)
            held2[t, fs] = meeting
            low, high = (
                pick(t, low, other_low) + coef2[0, t, fs] * meeting,
                pick(t, other_high, high) + coef2[1, t, fs] * meeting,
            )
            offer(step, t + 1, c, low, high)
            return
        middle = (low + other_low) * coef2[2, t, fs]
        top = high * coef2[1, t, fs] + coef2[0, t, fs] * middle
        base = pick(t, jnp.zeros_like(middle), middle)
        value = pick(t, middle, top)
        for r in range(last - 1, -1, -1):
            middle = (
                held2[r, fs] * coef2[2, r, fs] + coef2[0, r, fs] * base + coef2[1, r, fs] * value
            )
            base, value = pick(r, base, middle), pick(r, middle, value)
        back1[step, g1 - 1, fs, 1] = value
        for i in range(g1 - 1, 0, -1):
            value = (
                held1[i - 1, fs] * coef1[2, i - 1, fs]
                + coef1[0, i - 1, fs] * base
                + coef1[1, i - 1, fs] * value
            )
            back1[step, i, fs, 0] = value
            back1[step, i - 1, fs, 1] = value
        back1[step, 0, fs, 0] = base
        for offset in range(1, g1):
            in1(step, c, offset).start()
        home1[step, mine1, fs] = back1[step, mine1, fs]

    def own_backward(step, f):
        @pl.when(lax.rem(f, chunk) == 0)
        def arrive():
            c = lax.div(f, chunk)
            await_bytes(home1.at[step, pl.ds(0, g1 - 1), of_chunk(c)], b1_recv.at[step, c])

        for c in range(g1):
            cut = slice(c * TILE_LANES, (c + 1) * TILE_LANES)
            base = home1[step, c, f, 0]
            value = home1[step, c, f, 1]
            for k in range(layers - 1, -1, -1):
                if k < layers - 1:
                    value = (
                        held0[k, f, :, cut] * coef0[2, k, f, :, cut]
                        + coef0[0, k, f, :, cut] * base
                        + coef0[1, k, f, :, cut] * value
                    )
                if step == STEPS - 1:
                    result[f, k, :, cut] = value
                else:
                    present[step + 1, f, k, :rows, cut] = value
        if step < STEPS - 1:
            for copy in halos(step + 1, f):
                copy.start()
        else:
            field_out(f).start()

    def sent_out(step):
        await_bytes(present.at[step, :, :, pl.ds(0, 2 * EDGE)], halo_send.at[step])
        await_bytes(send1.at[step, pl.ds(0, g1 - 1)], s1_send.at[step])
        for t in range(rounds):
            await_bytes(send2.at[step, t, :, pl.ds(0, 1 if t == last else 2)], s2_send.at[step, t])

    def sent_home(step):
        await_bytes(back1.at[step, pl.ds(0, g1 - 1)], b1_send.at[step])

    each_field(functools.partial(own_forward, 0))
    await_bytes(rates_plane.at[pl.ds(0, g1 - 1)], rate_recv.at[0])
    plane_factors()
    for step in range(STEPS):
        each_chunk(functools.partial(plane_forward, step))
        for t in range(rounds):
            if step == 0:
                stack_factors(t)
            each_chunk(functools.partial(stack_round, step, t))
        if step == 0:
            await_bytes(speed.at[:, :, pl.ds(0, 2 * EDGE)], speed_send.at[0])
            await_bytes(rates_plane.at[pl.ds(0, g1 - 1)], rate_send.at[0])
            for t in range(rounds):
                await_bytes(send_el.at[t, :, pl.ds(0, 1 if t == last else 3)], el_send.at[t])
        sent_out(step)
        if step < STEPS - 1:
            own_backward(step, jnp.int32(0))

            def turn(f, carry, step=step):
                own_backward(step, f)
                own_forward(step + 1, f - 1)
                return carry

            lax.fori_loop(1, field_total, turn, 0)
            own_forward(step + 1, jnp.int32(field_total - 1))
            sent_home(step)
        else:
            each_field(functools.partial(own_backward, step))
            sent_home(step)
            each_field(lambda f: field_out(f).wait())


def on_device(fields, velocity, face_rate, xy_rate, z_scale):
    gz_count = lax.axis_size("gz")
    gy_count = lax.axis_size("gy")
    field_total, layers, rows, width = fields.shape
    g1 = width // TILE_LANES
    g2 = gz_count // g1
    rounds = g2.bit_length() - 1
    assert g1 * 2**rounds == gz_count
    chunk = 2 if field_total % 2 == 0 else 1
    plan = (g1, g2, rounds, gy_count, chunk)
    extent = rows + TILE_ROWS
    share1 = (rows, TILE_LANES)
    vmem = lambda *shape: pltpu.VMEM(shape, jnp.float32)
    dma = lambda *shape: pltpu.SemaphoreType.DMA(shape)
    return pl.pallas_call(
        functools.partial(kernel, plan),
        out_shape=jax.ShapeDtypeStruct(fields.shape, jnp.float32),
        in_specs=[pl.BlockSpec(memory_space=pl.ANY)] * 5,
        out_specs=pl.BlockSpec(memory_space=pl.ANY),
        scratch_shapes=[
            pltpu.SMEM((field_total,), jnp.float32),
            pltpu.SMEM((field_total,), jnp.float32),
            vmem(STEPS, field_total, layers, extent, width),
            vmem(2, layers, extent, width),
            vmem(layers, rows, width),
            vmem(g1, layers, rows, TILE_LANES),
            vmem(3, layers - 1, field_total, rows, width),
            vmem(layers - 1, field_total, rows, width),
            vmem(3, g1 - 1, field_total, *share1),
            vmem(g1 - 1, field_total, *share1),
            vmem(3, rounds, field_total, *share1),
            vmem(rounds, field_total, *share1),
            vmem(field_total, layers, rows, width),
            vmem(STEPS, g1, field_total, 2, *share1),
            vmem(STEPS, g1, field_total, 2, *share1),
            vmem(STEPS, g1, field_total, 2, *share1),
            vmem(STEPS, g1, field_total, 2, *share1),
            vmem(STEPS, rounds, field_total // chunk, 2, chunk, *share1),
            vmem(STEPS, rounds, field_total // chunk, 2, chunk, *share1),
            vmem(rounds, field_total, 3, *share1),
            vmem(rounds, field_total, 3, *share1),
            dma(5),
            dma(field_total),
            dma(field_total),
            dma(STEPS),
            dma(STEPS, field_total),
            dma(1),
            dma(1),
            dma(1),
            dma(1),
            dma(STEPS),
            dma(STEPS, field_total // chunk),
            dma(STEPS),
            dma(STEPS, field_total // chunk),
            dma(STEPS, rounds),
            dma(STEPS, rounds, field_total // chunk),
            dma(rounds),
            dma(rounds, field_total),
        ],
        compiler_params=pltpu.CompilerParams(
            collective_id=0, has_side_effects=True, vmem_limit_bytes=60 * 1024 * 1024
        ),
        cost_estimate=pl.CostEstimate(
            flops=400 * fields.size, bytes_accessed=16 * fields.size, transcendentals=0
        ),
    )(xy_rate, z_scale, fields, velocity, face_rate)


def solution(mesh):
    in_specs = (P(None, "gz", "gy", None), P(None, "gz", "gy", None), P("gz", "gy", None), P(), P())
    out_specs = P(None, "gz", "gy", None)
    return jax.shard_map(
        on_device, mesh=mesh, in_specs=in_specs, out_specs=out_specs, check_vma=False
    )
```

```python
import functools

import jax
import jax.numpy as jnp
from jax import lax
from jax.experimental import pallas as pl
from jax.experimental.pallas import tpu as pltpu
from jax.sharding import PartitionSpec as P

STEPS = 2
TILE_ROWS = 8
TILE_LANES = 128
EDGE = 2
MESH = pl.DeviceIdType.MESH


def stencil(q, north, south, weights):
    width = q.shape[1]
    east, west, up, down, centre = weights
    eastern = pltpu.roll(q, width - 1, 1)
    western = pltpu.roll(q, 1, 1)
    return (east * eastern + west * western) + (up * north + down * south) + centre * q


def reciprocal(value):
    estimate = pl.reciprocal(value, approx=True)
    estimate = estimate * (2.0 - value * estimate)
    return estimate * (2.0 - value * estimate)


def join(lower, upper):
    between = lower[2] + upper[1]
    inverse = reciprocal(lower[0] + upper[0] + between)
    to_low = lower[0] * inverse
    to_high = upper[0] * inverse
    element = (to_low * upper[0], lower[1] + to_low * between, upper[2] + to_high * between)
    return element, (to_low, to_high, inverse)


def layer_element(rate):
    return (rate, jnp.zeros_like(rate), jnp.ones_like(rate))


def kernel(
    plan,
    xy_hbm,
    z_hbm,
    fields,
    velocity,
    face_rate,
    out,
    xy_rate,
    z_scale,
    present,
    speed,
    rates,
    rates_plane,
    coef0,
    held0,
    coef1,
    held1,
    coef2,
    held2,
    result,
    send1,
    recv1,
    back1,
    home1,
    send2,
    recv2,
    send_el,
    recv_el,
    local_sem,
    field_sem,
    out_sem,
    halo_send,
    halo_recv,
    speed_send,
    speed_recv,
    rate_send,
    rate_recv,
    s1_send,
    s1_recv,
    b1_send,
    b1_recv,
    s2_send,
    s2_recv,
    el_send,
    el_recv,
):
    g1, g2, rounds, gy_count = plan
    field_total, layers, rows, width = fields.shape
    halo = TILE_ROWS
    me = lax.axis_index("gz")
    my_y = lax.axis_index("gy")
    mine1 = lax.rem(me, g1)
    mine2 = lax.div(me, g1)
    upper_y = lax.rem(my_y + 1, gy_count)
    lower_y = lax.rem(my_y + gy_count - 1, gy_count)

    def plane_peer(offset):
        return lax.rem(mine1 + offset, g1)

    def stack_bit(t):
        return lax.rem(lax.div(mine2, 2**t), 2)

    def stack_peer(t):
        return mine2 + (1 - 2 * stack_bit(t)) * 2**t

    def pick(t, lower, upper):
        return jnp.where(jnp.broadcast_to(stack_bit(t), lower.shape) == 0, lower, upper)

    def plane_id(position):
        return {"gz": mine2 * g1 + position}

    def stack_id(position):
        return {"gz": position * g1 + mine1}

    def lanes(position):
        return pl.ds(pl.multiple_of(position * TILE_LANES, TILE_LANES), TILE_LANES)

    def each_field(body):
        def step_body(f, carry):
            body(f)
            return carry

        lax.fori_loop(0, field_total, step_body, 0)

    def remote(source, target, send_sem, recv_sem, device):
        return pltpu.make_async_remote_copy(
            src_ref=source,
            dst_ref=target,
            send_sem=send_sem,
            recv_sem=recv_sem,
            device_id=device,
            device_id_type=MESH,
        )

    def await_bytes(ref, semaphore):
        pltpu.make_async_copy(ref, ref, semaphore).wait()

    def field_in(f):
        return pltpu.make_async_copy(
            fields.at[f], present.at[0, f, :, pl.ds(0, rows)], field_sem.at[f]
        )

    def field_out(f):
        return pltpu.make_async_copy(result.at[f], out.at[f], out_sem.at[f])

    for ref in (present, speed):
        ref[..., rows:, :] = jnp.zeros(ref.shape[:-2] + (halo, width), jnp.float32)

    locals_in = [
        pltpu.make_async_copy(z_hbm, z_scale, local_sem.at[0]),
        pltpu.make_async_copy(xy_hbm, xy_rate, local_sem.at[1]),
        pltpu.make_async_copy(face_rate, rates, local_sem.at[2]),
        pltpu.make_async_copy(velocity, speed.at[:, :, pl.ds(0, rows)], local_sem.at[3]),
        pltpu.make_async_copy(
            face_rate.at[:, :, lanes(mine1)], rates_plane.at[mine1], local_sem.at[4]
        ),
    ]
    for copy in locals_in:
        copy.start()
    each_field(lambda f: field_in(f).start())

    barrier = pltpu.get_barrier_semaphore()
    for target in (lower_y, upper_y):
        pl.semaphore_signal(barrier, inc=1, device_id={"gy": target}, device_id_type=MESH)
    for offset in range(1, g1):
        pl.semaphore_signal(
            barrier, inc=1, device_id=plane_id(plane_peer(offset)), device_id_type=MESH
        )
    for t in range(rounds):
        pl.semaphore_signal(
            barrier, inc=1, device_id=stack_id(stack_peer(t)), device_id_type=MESH
        )
    pl.semaphore_wait(barrier, 2 + g1 - 1 + rounds)

    def halo_pair(source, target, send_sem, recv_sem):
        return [
            remote(
                source.at[..., pl.ds(0, EDGE), :],
                target.at[..., pl.ds(rows, EDGE), :],
                send_sem,
                recv_sem,
                {"gy": lower_y},
            ),
            remote(
                source.at[..., pl.ds(rows - EDGE, EDGE), :],
                target.at[..., pl.ds(rows + halo - EDGE, EDGE), :],
                send_sem,
                recv_sem,
                {"gy": upper_y},
            ),
        ]

    def halos(step, f):
        source = fields.at[f] if step == 0 else present.at[step, f]
        return halo_pair(
            source, present.at[step, f], halo_send.at[step], halo_recv.at[step, f]
        )

    def rate_copy(offset):
        return remote(
            face_rate.at[:, :, lanes(plane_peer(offset))],
            rates_plane.at[mine1],
            rate_send.at[0],
            rate_recv.at[0],
            plane_id(plane_peer(offset)),
        )

    def out1(step, f, offset):
        return remote(
            send1.at[step, plane_peer(offset), f],
            recv1.at[step, mine1, f],
            s1_send.at[step],
            s1_recv.at[step, f],
            plane_id(plane_peer(offset)),
        )

    def in1(step, f, offset):
        return remote(
            back1.at[step, plane_peer(offset), f],
            home1.at[step, mine1, f],
            b1_send.at[step],
            b1_recv.at[step, f],
            plane_id(plane_peer(offset)),
        )

    last = rounds - 1

    def payload2(buffer, step, t, f):
        return buffer.at[step, t, f, pl.ds(0, 1 if t == last else 2)]

    def payload_el(buffer, t, f):
        return buffer.at[t, f, pl.ds(0, 1 if t == last else 3)]

    def pair2(step, t, f):
        return remote(
            payload2(send2, step, t, f),
            payload2(recv2, step, t, f),
            s2_send.at[step, t],
            s2_recv.at[step, t, f],
            stack_id(stack_peer(t)),
        )

    def pair_el(t, f):
        return remote(
            payload_el(send_el, t, f),
            payload_el(recv_el, t, f),
            el_send.at[t],
            el_recv.at[t, f],
            stack_id(stack_peer(t)),
        )

    speed_halos = halo_pair(velocity, speed, speed_send.at[0], speed_recv.at[0])
    for copy in speed_halos:
        copy.start()

    def start_halos(f):
        for copy in halos(0, f):
            copy.start()

    each_field(start_halos)
    for offset in range(1, g1):
        rate_copy(offset).start()

    for copy in locals_in[:3]:
        copy.wait()

    def own_factors(f):
        scale = z_scale[f]
        element = layer_element(scale * rates[0])
        for k in range(1, layers):
            element, factors = join(element, layer_element(scale * rates[k]))
            for n in range(3):
                coef0[n, k - 1, f] = factors[n]

    each_field(own_factors)

    for copy in locals_in[3:]:
        copy.wait()
    await_bytes(speed.at[:, :, pl.ds(0, 2 * EDGE)], speed_recv.at[0])
    for n in range(2):
        for k in range(layers):
            speed[n, k] = 0.5 * speed[n, k]

    def plane_factors():
        totals = []
        for f in range(field_total):
            scale = z_scale[f]
            total = None
            for i in range(g1):
                element = layer_element(scale * rates_plane[i, 0])
                for k in range(1, layers):
                    element, ignored = join(element, layer_element(scale * rates_plane[i, k]))
                if total is None:
                    total = element
                else:
                    total, factors = join(total, element)
                    for n in range(3):
                        coef1[n, i - 1, f] = factors[n]
            totals.append(total)
        for f in range(field_total):
            offer_element(0, f, totals[f])
        for f in range(field_total):
            pair_el(0, f).start()

    def offer_element(t, f, element):
        if t < last:
            for n in range(3):
                send_el[t, f, n] = element[n]
        else:
            closing = element[0] + element[2]
            inverse = reciprocal(closing)
            ratio = element[0] * inverse
            coef2[0, t, f] = ratio
            coef2[1, t, f] = inverse
            send_el[t, f, 0] = pick(t, closing, element[1] + ratio * element[2])

    def stack_factors(t):
        for f in range(field_total):
            await_bytes(payload_el(recv_el, t, f), el_recv.at[t, f])
        for f in range(field_total):
            stack_factors_of(t, f)
        if t < last:
            for f in range(field_total):
                pair_el(t + 1, f).start()

    def stack_factors_of(t, f):
        if t < last:
            mine = tuple(send_el[t, f, n] for n in range(3))
            other = tuple(recv_el[t, f, n] for n in range(3))
            lower = tuple(pick(t, a, b) for a, b in zip(mine, other))
            upper = tuple(pick(t, b, a) for a, b in zip(mine, other))
            total, factors = join(lower, upper)
            for n in range(3):
                coef2[n, t, f] = factors[n]
            offer_element(t + 1, f, total)
        else:
            coef2[2, t, f] = reciprocal(send_el[t, f, 0] + recv_el[t, f, 0])

    def own_forward(step, f):
        if step == 0:
            field_in(f).wait()
        await_bytes(present.at[step, f, :, pl.ds(0, 2 * EDGE)], halo_recv.at[step, f])
        spread = xy_rate[f]
        centre = 1.0 - 4.0 * spread
        low = None
        high = None
        extent = rows + halo
        for k in range(layers):
            q = present[step, f, k]
            along_x = speed[0, k]
            along_y = speed[1, k]
            weights = (
                spread - along_x,
                spread + along_x,
                spread - along_y,
                spread + along_y,
                centre,
            )
            sectioned = stencil(q, pltpu.roll(q, extent - 1, 0), pltpu.roll(q, 1, 0), weights)
            north = pltpu.roll(sectioned, extent - 1, 0)[:rows]
            south = pltpu.roll(sectioned, 1, 0)[:rows]
            inner_weights = tuple(w[:rows] for w in weights[:4]) + (centre,)
            explicit = 0.5 * (
                q[:rows] + stencil(sectioned[:rows], north, south, inner_weights)
            )
            if k == 0:
                high = explicit
            else:
                held0[k - 1, f] = high
                share = coef0[0, k - 1, f] * high
                low = share if low is None else low + share
                high = explicit + coef0[1, k - 1, f] * high
        for c in range(g1):
            cut = slice(c * TILE_LANES, (c + 1) * TILE_LANES)
            send1[step, c, f, 0] = low[:, cut]
            send1[step, c, f, 1] = high[:, cut]
        for offset in range(1, g1):
            out1(step, f, offset).start()
        recv1[step, mine1, f] = send1[step, mine1, f]

    def plane_forward(step, f):
        await_bytes(recv1.at[step, pl.ds(0, g1 - 1), f], s1_recv.at[step, f])
        low = recv1[step, 0, f, 0]
        high = recv1[step, 0, f, 1]
        for i in range(1, g1):
            meeting = high + recv1[step, i, f, 0]
            held1[i - 1, f] = meeting
            low = low + coef1[0, i - 1, f] * meeting
            high = recv1[step, i, f, 1] + coef1[1, i - 1, f] * meeting
        offer(step, 0, f, low, high)

    def offer(step, t, f, low, high):
        if t < last:
            send2[step, t, f, 0] = low
        else:
            send2[step, t, f, 0] = pick(t, high, low + coef2[0, t, f] * high)
        send2[step, t, f, 1] = high
        pair2(step, t, f).start()

    def stack_round(step, t, f):
        await_bytes(payload2(recv2, step, t, f), s2_recv.at[step, t, f])
        low = send2[step, t, f, 0]
        high = send2[step, t, f, 1]
        other_low = recv2[step, t, f, 0]
        if t < last:
            other_high = recv2[step, t, f, 1]
            meeting = pick(t, high, other_high) + pick(t, other_low, low)
            held2[t, f] = meeting
            low, high = (
                pick(t, low, other_low) + coef2[0, t, f] * meeting,
                pick(t, other_high, high) + coef2[1, t, f] * meeting,
            )
            offer(step, t + 1, f, low, high)
            return
        middle = (low + other_low) * coef2[2, t, f]
        top = high * coef2[1, t, f] + coef2[0, t, f] * middle
        base = pick(t, jnp.zeros_like(middle), middle)
        value = pick(t, middle, top)
        for r in range(last - 1, -1, -1):
            middle = (
                held2[r, f] * coef2[2, r, f] + coef2[0, r, f] * base + coef2[1, r, f] * value
            )
            base, value = pick(r, base, middle), pick(r, middle, value)
        back1[step, g1 - 1, f, 1] = value
        for i in range(g1 - 1, 0, -1):
            value = (
                held1[i - 1, f] * coef1[2, i - 1, f]
                + coef1[0, i - 1, f] * base
                + coef1[1, i - 1, f] * value
            )
            back1[step, i, f, 0] = value
            back1[step, i - 1, f, 1] = value
        back1[step, 0, f, 0] = base
        for offset in range(1, g1):
            in1(step, f, offset).start()
        home1[step, mine1, f] = back1[step, mine1, f]

    def own_backward(step, f):
        await_bytes(home1.at[step, pl.ds(0, g1 - 1), f], b1_recv.at[step, f])
        for c in range(g1):
            cut = slice(c * TILE_LANES, (c + 1) * TILE_LANES)
            base = home1[step, c, f, 0]
            value = home1[step, c, f, 1]
            for k in range(layers - 1, -1, -1):
                if k < layers - 1:
                    value = (
                        held0[k, f, :, cut] * coef0[2, k, f, :, cut]
                        + coef0[0, k, f, :, cut] * base
                        + coef0[1, k, f, :, cut] * value
                    )
                if step == STEPS - 1:
                    result[f, k, :, cut] = value
                else:
                    present[step + 1, f, k, :rows, cut] = value
        if step < STEPS - 1:
            for copy in halos(step + 1, f):
                copy.start()
        else:
            field_out(f).start()

    def sent_out(step):
        await_bytes(present.at[step, :, :, pl.ds(0, 2 * EDGE)], halo_send.at[step])
        await_bytes(send1.at[step, pl.ds(0, g1 - 1)], s1_send.at[step])
        for t in range(rounds):
            await_bytes(send2.at[step, t, :, pl.ds(0, 1 if t == last else 2)], s2_send.at[step, t])

    def sent_home(step):
        await_bytes(back1.at[step, pl.ds(0, g1 - 1)], b1_send.at[step])

    each_field(functools.partial(own_forward, 0))
    await_bytes(rates_plane.at[pl.ds(0, g1 - 1)], rate_recv.at[0])
    plane_factors()
    for step in range(STEPS):
        if step == 0:
            plane_forward(step, 0)
        lax.fori_loop(1, field_total, lambda f, carry: plane_forward(step, f) or carry, 0)
        for t in range(rounds):
            if step == 0:
                stack_factors(t)
            each_field(functools.partial(stack_round, step, t))
        if step == 0:
            await_bytes(speed.at[:, :, pl.ds(0, 2 * EDGE)], speed_send.at[0])
            await_bytes(rates_plane.at[pl.ds(0, g1 - 1)], rate_send.at[0])
            for t in range(rounds):
                await_bytes(send_el.at[t, :, pl.ds(0, 1 if t == last else 3)], el_send.at[t])
        sent_out(step)
        if step < STEPS - 1:
            own_backward(step, 0)

            def turn(f, carry, step=step):
                own_backward(step, f)
                own_forward(step + 1, f - 1)
                return carry

            lax.fori_loop(1, field_total, turn, 0)
            plane_forward(step + 1, 0)
            own_forward(step + 1, field_total - 1)
            sent_home(step)
        else:
            each_field(functools.partial(own_backward, step))
            sent_home(step)
            each_field(lambda f: field_out(f).wait())


def on_device(fields, velocity, face_rate, xy_rate, z_scale):
    gz_count = lax.axis_size("gz")
    gy_count = lax.axis_size("gy")
    field_total, layers, rows, width = fields.shape
    g1 = width // TILE_LANES
    g2 = gz_count // g1
    rounds = g2.bit_length() - 1
    assert g1 * 2**rounds == gz_count
    plan = (g1, g2, rounds, gy_count)
    extent = rows + TILE_ROWS
    share1 = (rows, TILE_LANES)
    vmem = lambda *shape: pltpu.VMEM(shape, jnp.float32)
    dma = lambda *shape: pltpu.SemaphoreType.DMA(shape)
    return pl.pallas_call(
        functools.partial(kernel, plan),
        out_shape=jax.ShapeDtypeStruct(fields.shape, jnp.float32),
        in_specs=[pl.BlockSpec(memory_space=pl.ANY)] * 5,
        out_specs=pl.BlockSpec(memory_space=pl.ANY),
        scratch_shapes=[
            pltpu.SMEM((field_total,), jnp.float32),
            pltpu.SMEM((field_total,), jnp.float32),
            vmem(STEPS, field_total, layers, extent, width),
            vmem(2, layers, extent, width),
            vmem(layers, rows, width),
            vmem(g1, layers, rows, TILE_LANES),
            vmem(3, layers - 1, field_total, rows, width),
            vmem(layers - 1, field_total, rows, width),
            vmem(3, g1 - 1, field_total, *share1),
            vmem(g1 - 1, field_total, *share1),
            vmem(3, rounds, field_total, *share1),
            vmem(rounds, field_total, *share1),
            vmem(field_total, layers, rows, width),
            vmem(STEPS, g1, field_total, 2, *share1),
            vmem(STEPS, g1, field_total, 2, *share1),
            vmem(STEPS, g1, field_total, 2, *share1),
            vmem(STEPS, g1, field_total, 2, *share1),
            vmem(STEPS, rounds, field_total, 2, *share1),
            vmem(STEPS, rounds, field_total, 2, *share1),
            vmem(rounds, field_total, 3, *share1),
            vmem(rounds, field_total, 3, *share1),
            dma(5),
            dma(field_total),
            dma(field_total),
            dma(STEPS),
            dma(STEPS, field_total),
            dma(1),
            dma(1),
            dma(1),
            dma(1),
            dma(STEPS),
            dma(STEPS, field_total),
            dma(STEPS),
            dma(STEPS, field_total),
            dma(STEPS, rounds),
            dma(STEPS, rounds, field_total),
            dma(rounds),
            dma(rounds, field_total),
        ],
        compiler_params=pltpu.CompilerParams(
            collective_id=0, has_side_effects=True, vmem_limit_bytes=60 * 1024 * 1024
        ),
        cost_estimate=pl.CostEstimate(
            flops=400 * fields.size, bytes_accessed=16 * fields.size, transcendentals=0
        ),
    )(xy_rate, z_scale, fields, velocity, face_rate)


def solution(mesh):
    in_specs = (P(None, "gz", "gy", None), P(None, "gz", "gy", None), P("gz", "gy", None), P(), P())
    out_specs = P(None, "gz", "gy", None)
    return jax.shard_map(
        on_device, mesh=mesh, in_specs=in_specs, out_specs=out_specs, check_vma=False
    )
```
